256 devices in a mesh: seq: 64 (over z, x, core), head: 4 (over y).
Axes of the slice: x: 4, y: 4, z: 8, core: 2. Of those that a mesh axis runs over, the one named last changes fastest.
Arguments:
- query: bfloat16 [8192, 4096], P('seq', 'head'), may hold values from -4.5 to 4.5
- keys: bfloat16 [8192, 4096], P('seq', 'head'), may hold values from -4.5 to 4.5
- values: bfloat16 [8192, 4096], P('seq', 'head'), may hold values from -60 to 60
- gain: float32 [4096], P('head'), may hold values from 0.5 to 1.5
- out_grad: bfloat16 [8192, 4096], P('seq', 'head'), may hold values from -8 to 8
Outputs:
- out: bfloat16 [8192, 4096], P('seq', 'head')
- query_grad: bfloat16 [8192, 4096], P('seq', 'head')
- key_grad: bfloat16 [8192, 4096], P('seq', 'head')
- value_grad: bfloat16 [8192, 4096], P('seq', 'head')
The draws below stay inside these ranges and needn't reach their ends.
All inputs are finite; a program needn't handle non-finite values.
Results may differ from the reference program's by a relative error of at most 0.04.
Values may be sent and summed in bfloat16 or wider, within the bound.
No kernel may reach another device: no remote copies, remote signals or barrier semaphores. Data moves between devices by JAX's collectives and lax.ppermute only.
A program may use at most 64 MiB of HBM per device.

```python
import math
from functools import reduce
import jax
import jax.numpy as jnp
from jax import lax

HEADS = 32
DH = 128
BLOCK = 128
LEVELS = 4
TOKENS = 8192


def column_signs(key):
    return jnp.where(jax.random.bernoulli(jax.random.fold_in(key, 202), 0.5, (HEADS * DH,)), 1.0, -1.0)


def column_scale():
    column = (jnp.arange(HEADS * DH) // DH).astype(jnp.float32) / (HEADS - 1)
    return 10.0 ** column


def token_smooth(key):
    run_length = 2 ** (LEVELS - 1)
    coarse_key = jax.random.fold_in(key, 11)
    jitter_key = jax.random.fold_in(key, 12)
    smooth = 1.3 * jax.random.truncated_normal(coarse_key, -3.0, 3.0, (TOKENS // run_length, HEADS * DH))
    jitter = 0.75 * jax.random.truncated_normal(jitter_key, -3.0, 3.0, (TOKENS, HEADS * DH))
    return jnp.clip(jnp.repeat(smooth, run_length, axis=0) + jitter, -4.5, 4.5)


def draw_query(key, part):
    key = jax.random.fold_in(key, 1)
    base = token_smooth(key)
    return base.astype(jnp.bfloat16)


def draw_keys(key, part):
    key = jax.random.fold_in(key, 2)
    base = token_smooth(key)
    return base.astype(jnp.bfloat16)


def draw_values(key, part):
    signs = column_signs(key)
    key = jax.random.fold_in(key, 3)
    scale = column_scale()
    base = jax.random.truncated_normal(key, -5.9, 5.9, (TOKENS, HEADS * DH)) * scale[None, :] + (0.03 * signs * scale)[None, :]
    return base.astype(jnp.bfloat16)


def draw_out_grad(key, part):
    key = jax.random.fold_in(key, 5)
    base = jax.random.truncated_normal(key, -5.5, 5.5, (TOKENS, HEADS * DH))
    return base.astype(jnp.bfloat16)


def setup_inputs(seed: int = 0) -> dict:
    key_of = jax.random.split(jax.random.key(seed), 6)
    return {
        "query": draw_query(jax.random.fold_in(key_of[5], 71), 0),
        "keys": draw_keys(jax.random.fold_in(key_of[5], 71), 0),
        "values": draw_values(jax.random.fold_in(key_of[5], 71), 0),
        "gain": jnp.clip(1.0 + 0.1 * jax.random.normal(key_of[3], (HEADS * DH,), jnp.float32), 0.5, 1.5),
        "out_grad": draw_out_grad(jax.random.fold_in(key_of[5], 71), 0),
    }


eps = 1e-06
floor_score = -1e+30

def rounded(x):
    return lax.optimization_barrier(x.astype(jnp.bfloat16)).astype(jnp.float32)

def pooled(x, level):
    if level == 0:
        return x
    return x.astype(jnp.float32).reshape(x.shape[0] >> level, 2 ** level, x.shape[1]).mean(axis=1).astype(jnp.bfloat16)

def pool_sum(x, level):
    return x.reshape((x.shape[0] >> level, 2 ** level) + x.shape[1:]).sum(axis=1)

def expand(x, level):
    return jnp.repeat(x, 2 ** level, axis=0)

def partner_blocks(x, level):
    count = x.shape[0] // BLOCK
    blocks = x.reshape((count, BLOCK) + x.shape[1:])
    if level == 0:
        zero = jnp.zeros_like(blocks[:1])
        left = jnp.concatenate([zero, blocks[:-1]], axis=0)
        right = jnp.concatenate([blocks[1:], zero], axis=0)
        return jnp.concatenate([left, blocks, right], axis=1)
    pairs = blocks.reshape((count // 2, 2, BLOCK) + x.shape[1:])
    return pairs[:, ::-1].reshape((count, BLOCK) + x.shape[1:])

def owner_rows(grad, level):
    count = grad.shape[0]
    if level == 0:
        left = grad[:, :BLOCK]
        centre = grad[:, BLOCK:2 * BLOCK]
        right = grad[:, 2 * BLOCK:]
        zero = jnp.zeros_like(centre[:1])
        own = centre + jnp.concatenate([left[1:], zero], axis=0) + jnp.concatenate([zero, right[:-1]], axis=0)
        return own.reshape((count * BLOCK,) + grad.shape[2:])
    pairs = grad.reshape((count // 2, 2, BLOCK) + grad.shape[2:])
    return pairs[:, ::-1].reshape((count * BLOCK,) + grad.shape[2:])

def key_valid(count, level):
    if level > 0:
        return jnp.ones((count, BLOCK), jnp.bool_)
    index = jnp.arange(count)
    left = jnp.broadcast_to((index > 0)[:, None], (count, BLOCK))
    right = jnp.broadcast_to((index < count - 1)[:, None], (count, BLOCK))
    return jnp.concatenate([left, jnp.ones((count, BLOCK), jnp.bool_), right], axis=1)

def level_weights(query_rows, key_rows, level):
    count = query_rows.shape[0] // BLOCK
    query_blocks = query_rows.reshape(count, BLOCK, DH).astype(jnp.float32)
    key_blocks = partner_blocks(key_rows, level).astype(jnp.float32)
    valid = key_valid(count, level)
    scores = jnp.einsum('nqd,nkd->nqk', query_blocks, key_blocks) * (1.0 / math.sqrt(DH))
    scores = jnp.where(valid[:, None, :], scores, floor_score)
    top = lax.optimization_barrier(jnp.max(scores, axis=2))
    weights = jnp.where(valid[:, None, :], jnp.exp(scores - top[..., None]), 0.0)
    return (weights, top.reshape(-1))

def head_forward(query_head, key_head, value_head):
    tops = []
    totals = []
    sums = []
    for level in range(LEVELS):
        weights, top = level_weights(pooled(query_head, level), pooled(key_head, level), level)
        value_blocks = partner_blocks(pooled(value_head, level), level).astype(jnp.float32)
        summed = jnp.einsum('nqk,nkd->nqd', rounded(weights), value_blocks).reshape(-1, DH)
        tops.append(expand(top, level))
        totals.append(expand(lax.optimization_barrier(jnp.sum(weights, axis=2)).reshape(-1), level))
        sums.append(expand(summed, level))
    best = reduce(jnp.maximum, tops)
    factors = [2.0 ** level * jnp.exp(tops[level] - best) for level in range(LEVELS)]
    total = reduce(jnp.add, [factors[level] * totals[level] for level in range(LEVELS)])
    numer = reduce(jnp.add, [factors[level][:, None] * sums[level] for level in range(LEVELS)])
    return ((numer / total[:, None]).astype(jnp.bfloat16), best, total)

def head_backward(query_head, key_head, value_head, grad_head, attn_head, best, total):
    grad_f = grad_head.astype(jnp.float32)
    dot = lax.optimization_barrier(jnp.sum(grad_f * attn_head.astype(jnp.float32), axis=1))
    tokens = query_head.shape[0]
    query_grad = jnp.zeros((tokens, DH), jnp.float32)
    key_grad = jnp.zeros((tokens, DH), jnp.float32)
    value_grad = jnp.zeros((tokens, DH), jnp.float32)
    for level in range(LEVELS):
        query_rows = pooled(query_head, level)
        key_rows = pooled(key_head, level)
        weights, top = level_weights(query_rows, key_rows, level)
        count = query_rows.shape[0] // BLOCK
        share = 2.0 ** level * jnp.exp(expand(top, level) - best) / total
        grad_rows = rounded(pool_sum(share[:, None] * grad_f, level)).reshape(count, BLOCK, DH)
        offset = pool_sum(share * dot, level).reshape(count, BLOCK)
        key_blocks = partner_blocks(key_rows, level).astype(jnp.float32)
        value_blocks = partner_blocks(pooled(value_head, level), level).astype(jnp.float32)
        query_blocks = query_rows.reshape(count, BLOCK, DH).astype(jnp.float32)
        value_part = jnp.einsum('nqk,nqd->nkd', rounded(weights), grad_rows)
        pressure = jnp.einsum('nqd,nkd->nqk', grad_rows, value_blocks)
        slope = rounded(weights * (pressure - offset[..., None]))
        query_part = jnp.einsum('nqk,nkd->nqd', slope, key_blocks) * (1.0 / math.sqrt(DH))
        key_part = jnp.einsum('nqk,nqd->nkd', slope, query_blocks) * (1.0 / math.sqrt(DH))
        query_grad = query_grad + expand(query_part.reshape(-1, DH), level) / 2.0 ** level
        key_grad = key_grad + expand(owner_rows(key_part, level), level) / 2.0 ** level
        value_grad = value_grad + expand(owner_rows(value_part, level), level) / 2.0 ** level
    return (query_grad, key_grad, value_grad)

def reference(query, keys, values, gain, out_grad):
    tokens = query.shape[0]

    def split(x):
        return x.reshape(tokens, HEADS, DH).transpose(1, 0, 2)

    def join(x):
        return x.transpose(1, 0, 2).reshape(tokens, HEADS * DH)
    attn, best, total = lax.map(lambda group: head_forward(group[0], group[1], group[2]), (split(query), split(keys), split(values)))
    flat = join(attn).astype(jnp.float32)
    inv = lax.rsqrt(lax.optimization_barrier(jnp.sum(flat * flat, axis=1)) / (HEADS * DH) + eps)
    out = (flat * inv[:, None] * gain).astype(jnp.bfloat16)
    scaled = out_grad.astype(jnp.float32) * gain
    inner = lax.optimization_barrier(jnp.sum(scaled * flat, axis=1))
    attn_grad = (inv[:, None] * scaled - flat * (inv * inv * inv * inner / (HEADS * DH))[:, None]).astype(jnp.bfloat16)
    query_grad, key_grad, value_grad = lax.map(lambda group: head_backward(group[0], group[1], group[2], group[3], group[4], group[5], group[6]), (split(query), split(keys), split(values), split(attn_grad), attn, best, total))
    return (out, join(query_grad).astype(jnp.bfloat16), join(key_grad).astype(jnp.bfloat16), join(value_grad).astype(jnp.bfloat16))
```

```python
import math

import jax
import jax.numpy as jnp
from jax import lax
from jax.experimental import pallas as pl
from jax.experimental.pallas import tpu as pltpu
from jax.sharding import PartitionSpec as P

DH = 128
BLOCK = 128
GROUP = 8
TOKENS = GROUP * BLOCK
COARSE = TOKENS // 2 + TOKENS // 4 + TOKENS // 8
START = {1: 0, 2: TOKENS // 2, 3: TOKENS // 2 + TOKENS // 4}
EPS = 1e-06
FLOOR = -1e30
SCALE = 1.0 / math.sqrt(DH)
VMEM = pl.BlockSpec(memory_space=pltpu.VMEM)
F32 = jnp.float32
BF16 = jnp.bfloat16


def call(kernel, outs, n_in, scratch=(), flops=0, nbytes=0):
    return pl.pallas_call(
        kernel,
        out_shape=[jax.ShapeDtypeStruct(s, d) for s, d in outs],
        in_specs=[VMEM] * n_in,
        out_specs=[VMEM] * len(outs),
        scratch_shapes=[pltpu.VMEM(s, d) for s, d in scratch],
        compiler_params=pltpu.CompilerParams(vmem_limit_bytes=48 * 1024 * 1024),
        cost_estimate=pl.CostEstimate(flops=flops, bytes_accessed=nbytes, transcendentals=0),
    )


def rows(b, n=1):
    return pl.ds(b * BLOCK, n * BLOCK)


def nt(a, b):
    return lax.dot_general(a, b, (((1,), (1,)), ((), ())), preferred_element_type=F32)


def nn(a, b):
    return lax.dot_general(a, b, (((1,), (0,)), ((), ())), preferred_element_type=F32)


def tn(a, b):
    return lax.dot_general(a, b, (((0,), (0,)), ((), ())), preferred_element_type=F32)


def member():
    return lax.rem(lax.axis_index("seq"), GROUP)


def group():
    return lax.div(lax.axis_index("seq"), GROUP)


def pack_kernel(q, k, v, d, *messages):
    me = member()
    for step, message in enumerate(messages):
        cols = pl.ds(pl.multiple_of((me ^ step) * DH, DH), DH)
        for i, x in enumerate((q, k, v, d)):
            message[i] = x[:, cols]


def assemble_kernel(*refs):
    parts, (q, k, v, d, qp, kp, vp, pair, other, f32) = refs[:GROUP], refs[GROUP:]
    me = member()
    odd = lax.rem(group(), 2)
    for step, part in enumerate(parts):
        at = pl.ds(pl.multiple_of((me ^ step) * BLOCK, BLOCK), BLOCK)
        for i, x in enumerate((q, k, v, d)):
            x[at, :] = part[i]
    for x, p in ((q, qp), (k, kp), (v, vp)):
        f32[...] = x[...].astype(F32)
        n = TOKENS
        for level in (1, 2, 3):
            n //= 2
            pooled = f32[pl.ds(0, n, 2), :] + f32[pl.ds(1, n, 2), :]
            p[pl.ds(START[level], n), :] = (pooled * 0.5**level).astype(BF16)
            f32[pl.ds(0, n), :] = pooled
    last = (GROUP - 1) * BLOCK
    near = pl.ds(pl.multiple_of((1 - odd) * last, BLOCK), BLOCK)
    far = pl.ds(pl.multiple_of(odd * last, BLOCK), BLOCK)
    pair[0] = k[near, :]
    pair[1] = v[near, :]
    pair[2] = kp[pl.ds(START[3], BLOCK), :]
    pair[3] = vp[pl.ds(START[3], BLOCK), :]
    other[0] = k[far, :]
    other[1] = v[far, :]


def extend(ext, x, pair, other, i):
    odd = lax.rem(group(), 2) == 1
    ext[rows(1, GROUP), :] = x[...]
    ext[rows(0), :] = jnp.where(odd, pair[i], other[i])
    ext[rows(GROUP + 1), :] = jnp.where(odd, other[i], pair[i])


def spread(scratch, x, n, times=2):
    for j in range(times):
        scratch[pl.ds(j, n, times), :] = x
    return scratch[pl.ds(0, n * times), :]


def row_sum(x):
    ones = jnp.ones((8, DH), BF16)
    high = x.astype(BF16)
    low = (x - high.astype(F32)).astype(BF16)
    return (nt(ones, high) + nt(ones, low))[:1]


def forward_kernel(
    q, k, v, d, qp, kp, vp, pair, other, gain,
    attn, stats, w0, wc, share, share1, share2,
    ext_k, ext_v, tops, totals, sums, up_m, up_t, up_s,
):
    z = group()
    extend(ext_k, k, pair, other, 0)
    extend(ext_v, v, pair, other, 1)

    def block(queries, keys, values, at, invalid=None):
        scores = nt(queries, keys) * SCALE
        if invalid is not None:
            side, bad = invalid
            lane = lax.broadcasted_iota(jnp.int32, scores.shape, 1) // BLOCK
            scores = jnp.where((lane == side) & bad, FLOOR, scores)
        top = jnp.max(scores, axis=1, keepdims=True)
        weights = jnp.exp(scores - top)
        rounded = weights.astype(BF16)
        tops[at, :] = jnp.broadcast_to(top, (BLOCK, DH))
        totals[at, :] = jnp.broadcast_to(jnp.sum(weights, axis=1, keepdims=True), (BLOCK, DH))
        sums[at, :] = nn(rounded, values)
        return rounded

    base = TOKENS // BLOCK
    for b in range(GROUP):
        invalid = (0, z == 0) if b == 0 else None
        if b == GROUP - 1:
            invalid = (2, z == lax.axis_size("seq") // GROUP - 1)
        w0[rows(b), :] = block(q[rows(b), :], ext_k[rows(b, 3), :], ext_v[rows(b, 3), :], rows(b), invalid)
    for c in range(6):
        w = block(qp[rows(c), :], kp[rows(c ^ 1), :], vp[rows(c ^ 1), :], rows(base + c))
        wc[rows(c), :] = w
    wc[rows(6), :] = block(qp[rows(6), :], pair[2], pair[3], rows(base + 6))

    at = rows(base + 6)
    m, t, s = tops[at, :], totals[at, :] * 8.0, sums[at, :] * 8.0
    n = TOKENS // 8
    for level, out in ((2, share2), (1, share1), (0, share)):
        em, et, es = spread(up_m, m, n), spread(up_t, t, n), spread(up_s, s, n)
        n *= 2
        at = pl.ds(TOKENS + START[level], n) if level else pl.ds(0, n)
        own = tops[at, :]
        m = jnp.maximum(own, em)
        here = 2.0**level * jnp.exp(own - m)
        up = jnp.exp(em - m)
        t = here * totals[at, :] + up * et
        s = here * sums[at, :] + up * es
        if level == 0:
            inverse = 1.0 / t
            here, up = here * inverse, up * inverse
            s = s * inverse
        out[0] = here
        out[1] = up
    rounded = s.astype(BF16)
    attn[...] = rounded
    flat = rounded.astype(F32)
    scaled = d[...].astype(F32) * gain[...]
    square = flat * flat
    inner = scaled * flat
    for b in range(GROUP):
        one = slice(b * BLOCK, (b + 1) * BLOCK)
        stats[0, pl.ds(b, 1), :] = row_sum(square[one])
        stats[1, pl.ds(b, 1), :] = row_sum(inner[one])


def backward_kernel(
    features,
    s0, s1, s2, s3, q, k, v, d, qp, kp, vp, pair, other, gain,
    attn, w0, wc, share, share1, share2,
    out, q_grad, k_grad, v_grad, pair_out, other_out,
    ext_k, ext_v, g0, gc, off0, offc, sl0, slc, buf, buf2, grads,
):
    odd = lax.rem(group(), 2) == 1
    extend(ext_k, k, pair, other, 0)
    extend(ext_v, v, pair, other, 1)
    sums = s0[...] + s1[...] + s2[...] + s3[...]
    inv_row = lax.rsqrt(sums[0] * (1.0 / features) + EPS)
    drop_row = inv_row * inv_row * inv_row * sums[1] * (1.0 / features)
    for b in range(GROUP):
        inv = jnp.broadcast_to(inv_row[b : b + 1], (BLOCK, DH)).T
        drop = jnp.broadcast_to(drop_row[b : b + 1], (BLOCK, DH)).T
        flat = attn[rows(b), :].astype(F32)
        scale_inv = inv * gain[...]
        out[rows(b), :] = (flat * scale_inv).astype(BF16)
        scaled = d[rows(b), :].astype(F32) * gain[...]
        grad = (inv * scaled - flat * drop).astype(BF16).astype(F32)
        dot = jnp.broadcast_to(jnp.sum(grad * flat, axis=1, keepdims=True), (BLOCK, DH))
        here, up = share[0, rows(b), :], share[1, rows(b), :]
        g0[rows(b), :] = (here * grad).astype(BF16)
        off0[rows(b), :] = here * dot
        buf[rows(b), :] = up * grad
        buf2[rows(b), :] = up * dot
    n = TOKENS
    for level, sh in ((1, share1), (2, share2), (3, None)):
        n //= 2
        g = buf[pl.ds(0, n, 2), :] + buf[pl.ds(1, n, 2), :]
        o = buf2[pl.ds(0, n, 2), :] + buf2[pl.ds(1, n, 2), :]
        at = pl.ds(START[level], n)
        if sh is None:
            gc[at, :] = (g * 8.0).astype(BF16)
            offc[at, :] = o * 8.0
        else:
            here, up = sh[0], sh[1]
            gc[at, :] = (g * here).astype(BF16)
            offc[at, :] = o * here
            buf[pl.ds(0, n), :] = g * up
            buf2[pl.ds(0, n), :] = o * up

    def block(grad, values, weights, offset, keys):
        pressure = nt(grad, values)
        wide = jnp.concatenate([offset] * (values.shape[0] // BLOCK), axis=1)
        slope = (weights.astype(F32) * (pressure - wide)).astype(BF16)
        return slope, nn(slope, keys) * SCALE

    for c in range(7):
        values = pair[3] if c == 6 else vp[rows(c ^ 1), :]
        keys = pair[2] if c == 6 else kp[rows(c ^ 1), :]
        slope, part = block(gc[rows(c), :], values, wc[rows(c), :], offc[rows(c), :], keys)
        slc[rows(c), :] = slope
        grads[rows(c), :] = part
    pair_out[2] = (tn(slc[rows(6), :], qp[rows(6), :]) * SCALE).astype(BF16)
    pair_out[3] = tn(wc[rows(6), :], gc[rows(6), :]).astype(BF16)
    e = grads[rows(6), :] * 0.125
    e = grads[rows(4, 2), :] * 0.25 + spread(buf, e, 128)
    e = grads[rows(0, 4), :] * 0.5 + spread(buf, e, 256)
    spread(buf, e, 512)
    for b in range(GROUP):
        slope, part = block(
            g0[rows(b), :], ext_v[rows(b, 3), :], w0[rows(b), :], off0[rows(b), :], ext_k[rows(b, 3), :]
        )
        sl0[rows(b), :] = slope
        q_grad[rows(b), :] = (part + buf[rows(b), :]).astype(BF16)

    def key_value(weight, factor, left, left_c, right, right_c, res):
        for c in range(6):
            grads[rows(c ^ 1), :] = tn(left_c[rows(c), :], right_c[rows(c), :])
        e = grads[rows(4, 2), :] * (0.25 * factor)
        e = grads[rows(0, 4), :] * (0.5 * factor) + spread(buf, e, 256)
        spread(buf, e, 512)
        edges = []
        for j in range(-1, GROUP + 1):
            total = None
            for side in range(3):
                b = j + 1 - side
                if 0 <= b < GROUP:
                    part = tn(left[rows(b), pl.ds(side * BLOCK, BLOCK)], right[rows(b), :])
                    total = part if total is None else total + part
            if 0 <= j < GROUP:
                res[rows(j), :] = total * factor + buf[rows(j), :]
            else:
                edges.append((total * factor).astype(BF16))
        pair_out[weight] = jnp.where(odd, edges[0], edges[1])
        other_out[weight] = jnp.where(odd, edges[1], edges[0])

    key_value(0, SCALE, sl0, slc, q, qp, k_grad)
    key_value(1, 1.0, w0, wc, g0, gc, v_grad)


def collect_kernel(out, q_grad, k_grad, v_grad, pair, other, *refs):
    messages, buf = refs[:-1], refs[-1]
    odd = lax.rem(group(), 2) == 1
    me = member()
    finished = []
    for i, x in enumerate((k_grad, v_grad)):
        spread(buf, pair[2 + i].astype(F32) * 0.125, 128, 8)
        buf[...] += x[...]
        buf[rows(0), :] += jnp.where(odd, pair[i], other[i]).astype(F32)
        buf[rows(GROUP - 1), :] += jnp.where(odd, other[i], pair[i]).astype(F32)
        for step, message in enumerate(messages):
            at = pl.ds(pl.multiple_of((me ^ step) * BLOCK, BLOCK), BLOCK)
            message[2 + i] = buf[at, :].astype(BF16)
    for step, message in enumerate(messages):
        at = pl.ds(pl.multiple_of((me ^ step) * BLOCK, BLOCK), BLOCK)
        message[0] = out[at, :]
        message[1] = q_grad[at, :]


def unpack_kernel(*refs):
    parts, results = refs[:GROUP], refs[GROUP:]
    me = member()
    for step, part in enumerate(parts):
        cols = pl.ds(pl.multiple_of((me ^ step) * DH, DH), DH)
        for i, x in enumerate(results):
            x[:, cols] = part[i]


def seq_permute(x, pairs):
    return lax.ppermute(x, "seq", pairs)


def swap(x, bits):
    return seq_permute(x, [(i, i ^ bits) for i in range(lax.axis_size("seq"))])


def swap_all(messages):
    result = [messages[0]] + [None] * (GROUP - 1)
    for step in (4, 5, 6, 7, 2, 3, 1):
        result[step] = swap(messages[step], step)
    return result


def swap_other(x):
    groups = lax.axis_size("seq") // GROUP
    up = [(g * GROUP + r, (g + 1) * GROUP + r) for g in range(1, groups - 1, 2) for r in range(GROUP)]
    return seq_permute(x, up + [(target, source) for source, target in up])


def local(query, keys, values, gain, out_grad):
    token = (BLOCK, query.shape[1])
    message = ((4, BLOCK, DH), BF16)
    edge = ((2, BLOCK, DH), BF16)
    whole = ((TOKENS, DH), BF16)
    whole_f = ((TOKENS, DH), F32)
    coarse = ((COARSE, DH), BF16)
    coarse_f = ((COARSE, DH), F32)
    extended = ((TOKENS + 2 * BLOCK, DH), BF16)
    wide = ((TOKENS, 3 * BLOCK), BF16)
    shares = [((2, TOKENS >> level, DH), F32) for level in range(3)]
    every = ((TOKENS + COARSE, DH), F32)
    features = query.shape[1] * lax.axis_size("head")

    my_gain = lax.dynamic_slice_in_dim(gain, (lax.axis_index("seq") % GROUP) * DH, DH).reshape(1, DH)
    packed = call(pack_kernel, [message] * GROUP, 4)(query, keys, values, out_grad)
    parts = swap_all(packed)
    q, k, v, d, qp, kp, vp, pair, other = call(
        assemble_kernel, [whole] * 4 + [coarse] * 3 + [message, edge], GROUP, [whole_f]
    )(*parts)
    pair, other = swap(pair, GROUP), swap_other(other)
    attn, stats, w0, wc, *share = call(
        forward_kernel,
        [whole, ((2, GROUP, DH), F32), wide, coarse] + shares,
        10,
        [extended] * 2 + [every] * 3 + [whole_f] * 3,
    )(q, k, v, d, qp, kp, vp, pair, other, my_gain)
    stats = stats + swap(stats, 1)
    stats = stats + swap(stats, 4) + swap(stats, 6) + swap(stats, 2)
    heads = lax.axis_size("head")
    stats = [stats] + [
        lax.ppermute(stats, "head", [(i, i ^ step) for i in range(heads)]) for step in (2, 3, 1)
    ]

    def backward(*refs):
        backward_kernel(features, *refs)

    out, q_grad, k_grad, v_grad, pair_back, other_back = call(
        backward,
        [whole, whole, whole_f, whole_f, message, edge],
        20,
        [extended] * 2 + [whole, coarse, whole_f, coarse_f, wide, coarse, whole_f, whole_f, coarse_f],
    )(*stats, q, k, v, d, qp, kp, vp, pair, other, my_gain, attn, w0, wc, *share)
    pair_back, other_back = swap(pair_back, GROUP), swap_other(other_back)
    messages = call(collect_kernel, [message] * GROUP, 6, [whole_f])(
        out, q_grad, k_grad, v_grad, pair_back, other_back
    )
    parts = swap_all(messages)
    return call(unpack_kernel, [(token, BF16)] * 4, GROUP)(*parts)


def solution(mesh):
    spec = P("seq", "head")
    in_specs = (spec, spec, spec, P("head"), spec)
    return jax.shard_map(
        local, mesh=mesh, in_specs=in_specs, out_specs=(spec,) * 4, check_vma=False
    )
```

```python
import math

import jax
import jax.numpy as jnp
from jax import lax
from jax.experimental import pallas as pl
from jax.experimental.pallas import tpu as pltpu
from jax.sharding import Mesh, PartitionSpec as P

DH = 128
BLOCK = 128
GROUP = 8
CHIPS = 4
HALF = CHIPS * 128
MID = GROUP - 2
TOKENS = GROUP * BLOCK
COARSE = TOKENS // 2 + TOKENS // 4 + TOKENS // 8
START = {1: 0, 2: TOKENS // 2, 3: TOKENS // 2 + TOKENS // 4}
EPS = 1e-06
FLOOR = -1e30
FLOPS = 4 * 10**9
SCALE = 1.0 / math.sqrt(DH)
VMEM = pl.BlockSpec(memory_space=pltpu.VMEM)
HBM = pl.BlockSpec(memory_space=pltpu.HBM)
F32 = jnp.float32
BF16 = jnp.bfloat16


def call(kernel, outs, ins, scratch=(), flops=0, vmem=16):
    return pl.pallas_call(
        kernel,
        out_shape=[jax.ShapeDtypeStruct(*out[:2]) for out in outs],
        in_specs=[VMEM] * ins if isinstance(ins, int) else ins,
        out_specs=[out[2] if len(out) > 2 else VMEM for out in outs],
        scratch_shapes=[pltpu.VMEM(*one) if isinstance(one, tuple) else one for one in scratch],
        compiler_params=pltpu.CompilerParams(vmem_limit_bytes=vmem * 1024 * 1024),
        cost_estimate=pl.CostEstimate(flops=flops, bytes_accessed=0, transcendentals=0),
    )


def run_all(copies):
    for copy in copies:
        copy.start()
    for copy in copies:
        copy.wait()


def at_block(b):
    return pl.ds(pl.multiple_of(b * BLOCK, BLOCK), BLOCK)


def rows(b, n=1):
    return pl.ds(b * BLOCK, n * BLOCK)


def nt(a, b):
    return lax.dot_general(a, b, (((1,), (1,)), ((), ())), preferred_element_type=F32)


def nn(a, b):
    return lax.dot_general(a, b, (((1,), (0,)), ((), ())), preferred_element_type=F32)


def tn(a, b):
    return lax.dot_general(a, b, (((0,), (0,)), ((), ())), preferred_element_type=F32)


def pack_kernel(x, y, got_x, got_y, *messages):
    core, chip = lax.axis_index("c"), lax.axis_index("x")
    mine, theirs = at_block(core), at_block(1 - core)
    for step, message in enumerate(messages):
        here = (chip ^ step) * DH
        cols = pl.ds(pl.multiple_of(core * HALF + here, DH), DH)
        for i, (own, got) in enumerate(((x, got_x), (y, got_y))):
            message[i, mine, :] = own[:, pl.ds(pl.multiple_of(here, DH), DH)]
            message[i, theirs, :] = got[:, cols]


def places():
    chip = lax.axis_index("x")
    return [pl.ds(pl.multiple_of((chip ^ step) * 2 * BLOCK, BLOCK), 2 * BLOCK) for step in range(CHIPS)]


def pool(x, p, f32):
    f32[...] = x[...].astype(F32)
    n = TOKENS
    for level in (1, 2, 3):
        n //= 2
        pooled = f32[pl.ds(0, n, 2), :] + f32[pl.ds(1, n, 2), :]
        p[pl.ds(START[level], n), :] = (pooled * 0.5**level).astype(BF16)
        f32[pl.ds(0, n), :] = pooled


def keys_kernel(*refs):
    parts, (k, v, kp, vp, pair, other, f32) = refs[:CHIPS], refs[CHIPS:]
    odd = lax.rem(lax.axis_index("z"), 2)
    for part, at in zip(parts, places()):
        k[at, :] = part[0]
        v[at, :] = part[1]
    pool(k, kp, f32)
    pool(v, vp, f32)
    near, far = at_block((1 - odd) * (GROUP - 1)), at_block(odd * (GROUP - 1))
    pair[0] = k[near, :]
    pair[1] = v[near, :]
    pair[2] = kp[pl.ds(START[3], BLOCK), :]
    pair[3] = vp[pl.ds(START[3], BLOCK), :]
    other[0] = k[far, :]
    other[1] = v[far, :]


def queries_kernel(*refs):
    parts, (q, d, qp, f32) = refs[:CHIPS], refs[CHIPS:]
    for part, at in zip(parts, places()):
        q[at, :] = part[0]
        d[at, :] = part[1]
    pool(q, qp, f32)


def spread(scratch, x, n, times=2):
    for j in range(times):
        scratch[pl.ds(j, n, times), :] = x
    return scratch[pl.ds(0, n * times), :]


def row_sum(x):
    ones = jnp.ones((8, DH), BF16)
    high = x.astype(BF16)
    low = (x - high.astype(F32)).astype(BF16)
    return (nt(ones, high) + nt(ones, low))[:1]


def attend(queries, keys, values, at, tops, totals, sums, invalid=None):
    scores = nt(queries, keys) * SCALE
    if invalid is not None:
        side, bad = invalid
        lane = lax.broadcasted_iota(jnp.int32, scores.shape, 1) // BLOCK
        scores = jnp.where((lane == side) & bad, FLOOR, scores)
    top = jnp.max(scores, axis=1, keepdims=True)
    weights = jnp.exp(scores - top)
    rounded = weights.astype(BF16)
    tops[at, :] = jnp.broadcast_to(top, (BLOCK, DH))
    totals[at, :] = jnp.broadcast_to(jnp.sum(weights, axis=1, keepdims=True), (BLOCK, DH))
    sums[at, :] = nn(rounded, values)
    return rounded


def forward_inner_kernel(q, k, v, qp, kp, vp, w_mid, w_coarse, tops, totals, sums):
    for b in range(MID):
        w_mid[rows(b), :] = attend(
            q[rows(b + 1), :], k[rows(b, 3), :], v[rows(b, 3), :], rows(b), tops, totals, sums
        )
    for c in range(6):
        w_coarse[rows(c), :] = attend(
            qp[rows(c), :], kp[rows(c ^ 1), :], vp[rows(c ^ 1), :], rows(MID + c), tops, totals, sums
        )


def forward_edge_kernel(
    q, k, v, d, qp, pair, other, gain, tops, totals, sums,
    attn, stats, w_edge, w_top, share, share1, share2, edge_k, edge_v,
    e_tops, e_totals, e_sums, up_m, up_t, up_s,
):
    z = lax.axis_index("z")
    odd = lax.rem(z, 2) == 1
    for x, edge, i in ((k, edge_k, 0), (v, edge_v, 1)):
        edge[0, rows(0), :] = jnp.where(odd, pair[i], other[i])
        edge[0, rows(1, 2), :] = x[rows(0, 2), :]
        edge[1, rows(0, 2), :] = x[rows(GROUP - 2, 2), :]
        edge[1, rows(2), :] = jnp.where(odd, other[i], pair[i])
    last = z == lax.axis_size("z") - 1
    for e, (b, invalid) in enumerate(((0, (0, z == 0)), (GROUP - 1, (2, last)))):
        w_edge[rows(e), :] = attend(
            q[rows(b), :], edge_k[e], edge_v[e], rows(e), e_tops, e_totals, e_sums, invalid
        )
    top3 = rows(2)
    w_top[...] = attend(qp[rows(6), :], pair[2], pair[3], top3, e_tops, e_totals, e_sums)
    m, t, s = e_tops[top3, :], e_totals[top3, :] * 8.0, e_sums[top3, :] * 8.0
    n = TOKENS // 8
    for level, out in ((2, share2), (1, share1)):
        em, et, es = spread(up_m, m, n), spread(up_t, t, n), spread(up_s, s, n)
        n *= 2
        at = pl.ds(MID * BLOCK + START[level], n)
        own = tops[at, :]
        m = jnp.maximum(own, em)
        here = 2.0**level * jnp.exp(own - m)
        up = jnp.exp(em - m)
        t = here * totals[at, :] + up * et
        s = here * sums[at, :] + up * es
        out[0] = here
        out[1] = up
    spread(up_m, m, n), spread(up_t, t, n), spread(up_s, s, n)
    for b in range(GROUP):
        if b in (0, GROUP - 1):
            at, (mm, tt, ss) = rows(b // (GROUP - 1)), (e_tops, e_totals, e_sums)
        else:
            at, (mm, tt, ss) = rows(b - 1), (tops, totals, sums)
        own, em = mm[at, :], up_m[rows(b), :]
        m = jnp.maximum(own, em)
        here, up = jnp.exp(own - m), jnp.exp(em - m)
        inverse = 1.0 / (here * tt[at, :] + up * up_t[rows(b), :])
        here, up = here * inverse, up * inverse
        rounded = (here * ss[at, :] + up * up_s[rows(b), :]).astype(BF16)
        share[0, rows(b), :] = here
        share[1, rows(b), :] = up
        attn[rows(b), :] = rounded
        flat = rounded.astype(F32)
        scaled = d[rows(b), :].astype(F32) * gain[...]
        sums_here = jnp.concatenate([row_sum(flat * flat), row_sum(scaled * flat)], axis=0)
        stats[:, :, pl.ds(b, 1), :] = jnp.broadcast_to(
            sums_here.reshape(1, 2, 1, BLOCK), (stats.shape[0], 2, 1, BLOCK)
        )


def slope_of(grad, values, weights, offset):
    pressure = nt(grad, values)
    wide = jnp.concatenate([offset] * (values.shape[0] // BLOCK), axis=1)
    return (weights.astype(F32) * (pressure - wide)).astype(BF16)


def backward_edge_kernel(
    features,
    stats, d, gain, attn, share, share1, share2, q, qp, pair, edge_k, edge_v, w_edge, w_top,
    out, pair_out, other_out, g0, gc, off0, offc, sl_edge, q_edge, q_top,
    buf, buf2,
):
    odd = lax.rem(lax.axis_index("z"), 2) == 1
    sums = jnp.sum(stats[...], axis=0) * (1.0 / features)
    inv_row = lax.rsqrt(sums[0] + EPS)
    drop_row = inv_row * inv_row * inv_row * sums[1]
    for b in range(GROUP):
        inv = jnp.broadcast_to(inv_row[b : b + 1], (BLOCK, DH)).T
        drop = jnp.broadcast_to(drop_row[b : b + 1], (BLOCK, DH)).T
        flat = attn[rows(b), :].astype(F32)
        out[rows(b), :] = (flat * (inv * gain[...])).astype(BF16)
        scaled = d[rows(b), :].astype(F32) * gain[...]
        grad = (inv * scaled - flat * drop).astype(BF16).astype(F32)
        dot = jnp.broadcast_to(jnp.sum(grad * flat, axis=1, keepdims=True), (BLOCK, DH))
        here, up = share[0, rows(b), :], share[1, rows(b), :]
        g0[rows(b), :] = (here * grad).astype(BF16)
        off0[rows(b), :] = here * dot
        buf[rows(b), :] = up * grad
        buf2[rows(b), :] = up * dot
    n = TOKENS
    for level, sh in ((1, share1), (2, share2), (3, None)):
        n //= 2
        g = buf[pl.ds(0, n, 2), :] + buf[pl.ds(1, n, 2), :]
        o = buf2[pl.ds(0, n, 2), :] + buf2[pl.ds(1, n, 2), :]
        at = pl.ds(START[level], n)
        if sh is None:
            gc[at, :] = (g * 8.0).astype(BF16)
            offc[at, :] = o * 8.0
        else:
            here, up = sh[0], sh[1]
            gc[at, :] = (g * here).astype(BF16)
            offc[at, :] = o * here
            buf[pl.ds(0, n), :] = g * up
            buf2[pl.ds(0, n), :] = o * up
    edges = []
    for e, b in ((0, 0), (1, GROUP - 1)):
        grad = g0[rows(b), :]
        slope = slope_of(grad, edge_v[e], w_edge[rows(e), :], off0[rows(b), :])
        sl_edge[rows(e), :] = slope
        q_edge[rows(e), :] = nn(slope, edge_k[e]) * SCALE
        side = slice(2 * e * BLOCK, (2 * e + 1) * BLOCK)
        edges.append((
            (tn(slope[:, side], q[rows(b), :]) * SCALE).astype(BF16),
            tn(w_edge[rows(e), side], grad).astype(BF16),
        ))
    grad = gc[rows(6), :]
    slope = slope_of(grad, pair[3], w_top[...], offc[rows(6), :])
    q_top[...] = nn(slope, pair[2]) * SCALE
    pair_out[2] = (tn(slope, qp[rows(6), :]) * SCALE).astype(BF16)
    pair_out[3] = tn(w_top[...], grad).astype(BF16)
    for i in range(2):
        pair_out[i] = jnp.where(odd, edges[0][i], edges[1][i])
        other_out[i] = jnp.where(odd, edges[1][i], edges[0][i])


def backward_inner_kernel(
    q, k, v, qp, kp, vp, w_mid, w_coarse, w_edge, g0, gc, off0, offc, sl_edge, q_edge, q_top,
    q_grad, k_grad, v_grad,
    sl_mid, sl_coarse, buf, grads,
):
    for c in range(6):
        slope = slope_of(gc[rows(c), :], vp[rows(c ^ 1), :], w_coarse[rows(c), :], offc[rows(c), :])
        sl_coarse[rows(c), :] = slope
        grads[rows(c), :] = nn(slope, kp[rows(c ^ 1), :]) * SCALE
    e = grads[rows(4, 2), :] * 0.25 + spread(buf, q_top[...] * 0.125, 128)
    e = grads[rows(0, 4), :] * 0.5 + spread(buf, e, 256)
    spread(buf, e, 512)
    for b in range(GROUP):
        if b in (0, GROUP - 1):
            part = q_edge[rows(b // (GROUP - 1)), :]
        else:
            slope = slope_of(
                g0[rows(b), :], v[rows(b - 1, 3), :], w_mid[rows(b - 1), :], off0[rows(b), :]
            )
            sl_mid[rows(b - 1), :] = slope
            part = nn(slope, k[rows(b - 1, 3), :]) * SCALE
        q_grad[rows(b), :] = (part + buf[rows(b), :]).astype(BF16)

    def key_value(factor, edge, mid, mid_c, right, right_c, res):
        for c in range(6):
            grads[rows(c ^ 1), :] = tn(mid_c[rows(c), :], right_c[rows(c), :])
        e = grads[rows(4, 2), :] * (0.25 * factor)
        e = grads[rows(0, 4), :] * (0.5 * factor) + spread(buf, e, 256)
        spread(buf, e, 512)
        for j in range(GROUP):
            total = None
            for side in range(3):
                b = j + 1 - side
                cols = pl.ds(side * BLOCK, BLOCK)
                if b in (0, GROUP - 1):
                    left = edge[rows(b // (GROUP - 1)), cols]
                elif 0 < b < GROUP - 1:
                    left = mid[rows(b - 1), cols]
                else:
                    continue
                part = tn(left, right[rows(b), :])
                total = part if total is None else total + part
            res[rows(j), :] = total * factor + buf[rows(j), :]

    key_value(SCALE, sl_edge, sl_mid, sl_coarse, q, qp, k_grad)
    key_value(1.0, w_edge, w_mid, w_coarse, g0, gc, v_grad)


def collect_kernel(out, q_grad, k_grad, v_grad, pair, other, *refs):
    messages, buf = refs[:-1], refs[-1]
    odd = lax.rem(lax.axis_index("z"), 2) == 1
    for i, x in enumerate((k_grad, v_grad)):
        spread(buf, pair[2 + i].astype(F32) * 0.125, 128, 8)
        buf[...] += x[...]
        buf[rows(0), :] += jnp.where(odd, pair[i], other[i]).astype(F32)
        buf[rows(GROUP - 1), :] += jnp.where(odd, other[i], pair[i]).astype(F32)
        for at, message in zip(places(), messages):
            message[2 + i] = buf[at, :].astype(BF16)
    for at, message in zip(places(), messages):
        message[0] = out[at, :]
        message[1] = q_grad[at, :]


def regroup_kernel(*refs):
    parts, (own, away) = refs[:CHIPS], refs[CHIPS:]
    core, chip = lax.axis_index("c"), lax.axis_index("x")
    mine, theirs = at_block(core), at_block(1 - core)
    for step, part in enumerate(parts):
        cols = pl.ds(pl.multiple_of((chip ^ step) * DH, DH), DH)
        for i in range(4):
            own[i, :, cols] = part[i, mine, :]
            away[i, :, cols] = part[i, theirs, :]


def finish_kernel(own, got, *refs):
    results, sem = refs[:-1], refs[-1]
    core = lax.axis_index("c")
    copies = []
    for i, x in enumerate(results):
        for j, (half, source) in enumerate(((1 - core, got), (core, own))):
            cols = pl.ds(pl.multiple_of(half * HALF, HALF), HALF)
            copies.append(pltpu.make_async_copy(source.at[i], x.at[:, cols], sem.at[j, i]))
    run_all(copies)


def swap_pair(x):
    return lax.ppermute(x, "z", [(i, i ^ 1) for i in range(lax.axis_size("z"))])


def swap_other(x):
    up = [(i, i + 1) for i in range(1, lax.axis_size("z") - 1, 2)]
    return lax.ppermute(x, "z", up + [(target, source) for source, target in up])


def swap_core(x):
    return lax.ppermute(x, "c", [(0, 1), (1, 0)])


def swap_chips(messages):
    return [messages[0]] + [
        lax.ppermute(messages[step], "x", [(i, i ^ step) for i in range(CHIPS)]) for step in (1, 2, 3)
    ]


def exchange(x, axes):
    return lax.all_to_all(x, axes, 0, 0, tiled=True)


def local(query, keys, values, gain, out_grad):
    token = ((BLOCK, query.shape[1]), BF16, HBM)
    part = ((2, 2 * BLOCK, DH), BF16)
    chip_part = ((4, 2 * BLOCK, DH), BF16)
    half = ((4, BLOCK, HALF), BF16)
    partners = GROUP * lax.axis_size("head")
    message = ((4, BLOCK, DH), BF16)
    edge = ((2, BLOCK, DH), BF16)
    whole = ((TOKENS, DH), BF16)
    whole_f = ((TOKENS, DH), F32)
    coarse = ((COARSE, DH), BF16)
    coarse_f = ((COARSE, DH), F32)
    one_f = ((BLOCK, DH), F32)
    two_f = ((2 * BLOCK, DH), F32)
    w_mids = ((MID * BLOCK, 3 * BLOCK), BF16)
    w_coarses = ((6 * BLOCK, BLOCK), BF16)
    w_edges = ((2 * BLOCK, 3 * BLOCK), BF16)
    w_tops = ((BLOCK, BLOCK), BF16)
    inner_f = (((MID + 6) * BLOCK, DH), F32)
    edge_sets = ((2, 3 * BLOCK, DH), BF16)
    shares = [((2, TOKENS >> level, DH), F32) for level in range(3)]
    features = query.shape[1] * lax.axis_size("head")

    head = lax.axis_index("c") * CHIPS + lax.axis_index("x")
    my_gain = lax.dynamic_slice_in_dim(gain, head * DH, DH).reshape(1, DH)

    def send(x, y):
        gots = [swap_core(one) for one in (x, y)]
        own = [lax.dynamic_slice_in_dim(one, lax.axis_index("c") * HALF, HALF, 1) for one in (x, y)]
        return swap_chips(call(pack_kernel, [part] * CHIPS, 4)(*own, *gots))

    got_keys = send(keys, values)
    got_queries = send(query, out_grad)
    k, v, kp, vp, pair, other = call(
        keys_kernel, [whole] * 2 + [coarse] * 2 + [message, edge], CHIPS, [whole_f]
    )(*got_keys)
    pair, other = swap_pair(pair), swap_other(other)
    q, d, qp = call(queries_kernel, [whole] * 2 + [coarse], CHIPS, [whole_f])(*got_queries)
    w_mid, w_coarse, *inner = call(
        forward_inner_kernel, [w_mids, w_coarses] + [inner_f] * 3, 6, flops=FLOPS
    )(q, k, v, qp, kp, vp)
    attn, stats, w_edge, w_top, share, share1, share2, edge_k, edge_v = call(
        forward_edge_kernel,
        [whole, ((partners, 2, GROUP, DH), F32), w_edges, w_tops] + shares + [edge_sets] * 2,
        11,
        [((3 * BLOCK, DH), F32)] * 3 + [whole_f] * 3,
    )(q, k, v, d, qp, pair, other, my_gain, *inner)
    stats = exchange(stats, ("x", "c", "head"))

    def backward_edge(*refs):
        backward_edge_kernel(features, *refs)

    out, pair_back, other_back, g0, gc, off0, offc, sl_edge, q_edge, q_top = call(
        backward_edge,
        [whole, message, edge, whole, coarse, whole_f, coarse_f, w_edges, two_f, one_f],
        14,
        [whole_f] * 2,
    )(stats, d, my_gain, attn, share, share1, share2, q, qp, pair, edge_k, edge_v, w_edge, w_top)
    pair_back, other_back = swap_pair(pair_back), swap_other(other_back)
    grads = call(
        backward_inner_kernel,
        [whole, whole_f, whole_f],
        16,
        [w_mids, w_coarses, whole_f, coarse_f],
        flops=2 * FLOPS,
    )(q, k, v, qp, kp, vp, w_mid, w_coarse, w_edge, g0, gc, off0, offc, sl_edge, q_edge, q_top)
    messages = call(collect_kernel, [chip_part] * CHIPS, 6, [whole_f])(
        out, *grads, pair_back, other_back
    )
    own, away = call(regroup_kernel, [half] * 2, CHIPS)(*swap_chips(messages))
    return call(finish_kernel, [token] * 4, 2, [pltpu.SemaphoreType.DMA((2, 4))])(own, swap_core(away))


def solution(mesh):
    chips = (CHIPS, 2)
    axes = ("z", "x", "c", "head")
    heads = mesh.shape["head"]
    fine = Mesh(mesh.devices.reshape((mesh.shape["seq"] // GROUP, *chips, heads)), axes)
    spec = P(("z", "x", "c"), "head")
    in_specs = (spec, spec, spec, P("head"), spec)
    return jax.shard_map(
        local, mesh=fine, in_specs=in_specs, out_specs=(spec,) * 4, check_vma=False
    )
```

```python
import math

import jax
import jax.numpy as jnp
from jax import lax
from jax.experimental import pallas as pl
from jax.experimental.pallas import tpu as pltpu
from jax.sharding import Mesh, PartitionSpec as P

DH = 128
BLOCK = 128
GROUP = 8
CHIPS = 4
STEPS = (0, 2, 3, 1)
HALF = CHIPS * 128
MID = GROUP - 2
TOKENS = GROUP * BLOCK
COARSE = TOKENS // 2 + TOKENS // 4 + TOKENS // 8
START = {1: 0, 2: TOKENS // 2, 3: TOKENS // 2 + TOKENS // 4}
EPS = 1e-06
FLOOR = -1e30
FLOPS = 4 * 10**9
SCALE = 1.0 / math.sqrt(DH)
SHARP = SCALE * math.log2(math.e)
VMEM = pl.BlockSpec(memory_space=pltpu.VMEM)
HBM = pl.BlockSpec(memory_space=pltpu.HBM)
F32 = jnp.float32
BF16 = jnp.bfloat16


def call(kernel, outs, ins, scratch=(), flops=0, vmem=16):
    return pl.pallas_call(
        kernel,
        out_shape=[jax.ShapeDtypeStruct(*out[:2]) for out in outs],
        in_specs=[VMEM] * ins if isinstance(ins, int) else ins,
        out_specs=[out[2] if len(out) > 2 else VMEM for out in outs],
        scratch_shapes=[pltpu.VMEM(*one) if isinstance(one, tuple) else one for one in scratch],
        compiler_params=pltpu.CompilerParams(vmem_limit_bytes=vmem * 1024 * 1024),
        cost_estimate=pl.CostEstimate(flops=flops, bytes_accessed=0, transcendentals=0),
    )


def run_all(copies):
    for copy in copies:
        copy.start()
    for copy in copies:
        copy.wait()


def at_block(b):
    return pl.ds(pl.multiple_of(b * BLOCK, BLOCK), BLOCK)


def rows(b, n=1):
    return pl.ds(b * BLOCK, n * BLOCK)


def nt(a, b):
    return lax.dot_general(a, b, (((1,), (1,)), ((), ())), preferred_element_type=F32)


def nn(a, b):
    return lax.dot_general(a, b, (((1,), (0,)), ((), ())), preferred_element_type=F32)


def tn(a, b):
    return lax.dot_general(a, b, (((0,), (0,)), ((), ())), preferred_element_type=F32)


def pack_kernel(x, y, got_x, got_y, *messages):
    core, chip = lax.axis_index("c"), lax.axis_index("x")
    mine, theirs = at_block(core), at_block(1 - core)
    for step, message in zip(STEPS, messages):
        here = (chip ^ step) * DH
        cols = pl.ds(pl.multiple_of(core * HALF + here, DH), DH)
        for i, (own, got) in enumerate(((x, got_x), (y, got_y))):
            message[i, mine, :] = own[:, pl.ds(pl.multiple_of(here, DH), DH)]
            message[i, theirs, :] = got[:, cols]


def places():
    chip = lax.axis_index("x")
    return [pl.ds(pl.multiple_of((chip ^ step) * 2 * BLOCK, BLOCK), 2 * BLOCK) for step in STEPS]


def pool(x, p, f32):
    f32[...] = x[...].astype(F32)
    n = TOKENS
    for level in (1, 2, 3):
        n //= 2
        pooled = f32[pl.ds(0, n, 2), :] + f32[pl.ds(1, n, 2), :]
        p[pl.ds(START[level], n), :] = (pooled * 0.5**level).astype(BF16)
        f32[pl.ds(0, n), :] = pooled


def keys_kernel(*refs):
    parts, (k, v, kp, vp, pair, other, f32) = refs[:CHIPS], refs[CHIPS:]
    odd = lax.rem(lax.axis_index("z"), 2)
    for part, at in zip(parts, places()):
        k[at, :] = part[0]
        v[at, :] = part[1]
    pool(k, kp, f32)
    pool(v, vp, f32)
    near, far = at_block((1 - odd) * (GROUP - 1)), at_block(odd * (GROUP - 1))
    pair[0] = k[near, :]
    pair[1] = v[near, :]
    pair[2] = kp[pl.ds(START[3], BLOCK), :]
    pair[3] = vp[pl.ds(START[3], BLOCK), :]
    other[0] = k[far, :]
    other[1] = v[far, :]


def queries_kernel(*refs):
    parts, (q, d, qp, f32) = refs[:CHIPS], refs[CHIPS:]
    for part, at in zip(parts, places()):
        q[at, :] = part[0]
        d[at, :] = part[1]
    pool(q, qp, f32)


def spread(scratch, x, n, times=2):
    for j in range(times):
        scratch[pl.ds(j, n, times), :] = x
    return scratch[pl.ds(0, n * times), :]


def column(x):
    return jnp.sum(x, axis=1, keepdims=True)


def attend(items, tops, totals, sums):
    scores = []
    for queries, keys, _, _, invalid in items:
        one = nt(queries, keys)
        if invalid is not None:
            side, bad = invalid
            lane = lax.broadcasted_iota(jnp.int32, one.shape, 1) // BLOCK
            one = jnp.where((lane == side) & bad, FLOOR, one)
        scores.append(one)
    weights = []
    for one, (_, _, _, at, _) in zip(scores, items):
        top = jnp.max(one, axis=1, keepdims=True)
        tops[at, :] = jnp.broadcast_to(top, (BLOCK, DH))
        weights.append(jnp.exp2((one - top) * SHARP))
    rounded = [one.astype(BF16) for one in weights]
    for one, (_, _, values, at, _) in zip(rounded, items):
        both = nn(one, jnp.concatenate([values, jnp.ones_like(values)], axis=1))
        sums[at, :] = both[:, :DH]
        totals[at, :] = both[:, DH:]
    return rounded


def forward_inner_kernel(q, k, v, qp, kp, vp, w_mid, w_coarse, tops, totals, sums):
    inner = [
        (q[rows(b + 1), :], k[rows(b, 3), :], v[rows(b, 3), :], rows(b), None) for b in range(MID)
    ]
    for b, one in enumerate(attend(inner, tops, totals, sums)):
        w_mid[rows(b), :] = one
    coarse = [
        (qp[rows(c), :], kp[rows(c ^ 1), :], vp[rows(c ^ 1), :], rows(MID + c), None) for c in range(6)
    ]
    for c, one in enumerate(attend(coarse, tops, totals, sums)):
        w_coarse[rows(c), :] = one


def forward_edge_kernel(
    q, k, v, d, qp, pair, other, gain, tops, totals, sums,
    attn, stats, w_edge, w_top, share, share1, share2, edge_k, edge_v,
    e_tops, e_totals, e_sums, up_m, up_t, up_s,
):
    z = lax.axis_index("z")
    odd = lax.rem(z, 2) == 1
    for x, edge, i in ((k, edge_k, 0), (v, edge_v, 1)):
        edge[0, rows(0), :] = jnp.where(odd, pair[i], other[i])
        edge[0, rows(1, 2), :] = x[rows(0, 2), :]
        edge[1, rows(0, 2), :] = x[rows(GROUP - 2, 2), :]
        edge[1, rows(2), :] = jnp.where(odd, other[i], pair[i])
    last = z == lax.axis_size("z") - 1
    top3 = rows(2)
    items = [
        (q[rows(b), :], edge_k[e], edge_v[e], rows(e), invalid)
        for e, (b, invalid) in enumerate(((0, (0, z == 0)), (GROUP - 1, (2, last))))
    ]
    items.append((qp[rows(6), :], pair[2], pair[3], top3, None))
    w_edge[rows(0), :], w_edge[rows(1), :], w_top[...] = attend(items, e_tops, e_totals, e_sums)
    m, t, s = e_tops[top3, :], e_totals[top3, :] * 8.0, e_sums[top3, :] * 8.0
    n = TOKENS // 8
    for level, out in ((2, share2), (1, share1)):
        em, et, es = spread(up_m, m, n), spread(up_t, t, n), spread(up_s, s, n)
        n *= 2
        at = pl.ds(MID * BLOCK + START[level], n)
        own = tops[at, :]
        m = jnp.maximum(own, em)
        here = 2.0**level * jnp.exp2((own - m) * SHARP)
        up = jnp.exp2((em - m) * SHARP)
        t = here * totals[at, :] + up * et
        s = here * sums[at, :] + up * es
        out[0] = here
        out[1] = up
    spread(up_m, m, n), spread(up_t, t, n), spread(up_s, s, n)
    lane = lax.broadcasted_iota(jnp.int32, (BLOCK, DH), 1)
    columns = jnp.zeros((BLOCK, DH), F32)
    for b in range(GROUP):
        if b in (0, GROUP - 1):
            at, (mm, tt, ss) = rows(b // (GROUP - 1)), (e_tops, e_totals, e_sums)
        else:
            at, (mm, tt, ss) = rows(b - 1), (tops, totals, sums)
        own, em = mm[at, :], up_m[rows(b), :]
        m = jnp.maximum(own, em)
        here, up = jnp.exp2((own - m) * SHARP), jnp.exp2((em - m) * SHARP)
        inverse = 1.0 / (here * tt[at, :] + up * up_t[rows(b), :])
        here, up = here * inverse, up * inverse
        rounded = (here * ss[at, :] + up * up_s[rows(b), :]).astype(BF16)
        share[0, rows(b), :] = here
        share[1, rows(b), :] = up
        attn[rows(b), :] = rounded
        flat = rounded.astype(F32)
        scaled = d[rows(b), :].astype(F32) * gain[...]
        for i, one in enumerate((column(flat * flat), column(scaled * flat))):
            columns = jnp.where(lane == i * GROUP + b, one, columns)
    turned = columns.T[: 2 * GROUP].reshape(1, 2, GROUP, BLOCK)
    stats[...] = jnp.broadcast_to(turned, stats.shape)


def slopes_of(items):
    pressures = [nt(grad, values) for grad, values, _, _ in items]
    slopes = []
    for pressure, (_, values, weights, offset) in zip(pressures, items):
        wide = jnp.concatenate([offset] * (values.shape[0] // BLOCK), axis=1)
        slopes.append((weights.astype(F32) * (pressure - wide)).astype(BF16))
    return slopes


def backward_edge_kernel(
    features,
    stats, d, gain, attn, share, share1, share2, q, qp, pair, edge_k, edge_v, w_edge, w_top,
    out, pair_out, other_out, g0, gc, off0, offc, sl_edge, q_edge, q_top,
    buf, buf2,
):
    odd = lax.rem(lax.axis_index("z"), 2) == 1
    sums = jnp.sum(stats[...], axis=0) * (1.0 / features)
    inv_row = lax.rsqrt(sums[0] + EPS)
    drop_row = inv_row * inv_row * inv_row * sums[1]
    for b in range(GROUP):
        inv = jnp.broadcast_to(inv_row[b : b + 1], (BLOCK, DH)).T
        drop = jnp.broadcast_to(drop_row[b : b + 1], (BLOCK, DH)).T
        flat = attn[rows(b), :].astype(F32)
        out[rows(b), :] = (flat * (inv * gain[...])).astype(BF16)
        scaled = d[rows(b), :].astype(F32) * gain[...]
        grad = (inv * scaled - flat * drop).astype(BF16).astype(F32)
        dot = jnp.broadcast_to(column(grad * flat), (BLOCK, DH))
        here, up = share[0, rows(b), :], share[1, rows(b), :]
        g0[rows(b), :] = (here * grad).astype(BF16)
        off0[rows(b), :] = here * dot
        buf[rows(b), :] = up * grad
        buf2[rows(b), :] = up * dot
    n = TOKENS
    for level, sh in ((1, share1), (2, share2), (3, None)):
        n //= 2
        g = buf[pl.ds(0, n, 2), :] + buf[pl.ds(1, n, 2), :]
        o = buf2[pl.ds(0, n, 2), :] + buf2[pl.ds(1, n, 2), :]
        at = pl.ds(START[level], n)
        if sh is None:
            gc[at, :] = (g * 8.0).astype(BF16)
            offc[at, :] = o * 8.0
        else:
            here, up = sh[0], sh[1]
            gc[at, :] = (g * here).astype(BF16)
            offc[at, :] = o * here
            buf[pl.ds(0, n), :] = g * up
            buf2[pl.ds(0, n), :] = o * up
    items = [
        (g0[rows(b), :], edge_v[e], w_edge[rows(e), :], off0[rows(b), :])
        for e, b in ((0, 0), (1, GROUP - 1))
    ]
    top_grad = gc[rows(6), :]
    items.append((top_grad, pair[3], w_top[...], offc[rows(6), :]))
    slopes = slopes_of(items)
    edges = []
    for e, b in ((0, 0), (1, GROUP - 1)):
        sl_edge[rows(e), :] = slopes[e]
        q_edge[rows(e), :] = nn(slopes[e], edge_k[e]) * SCALE
        side = slice(2 * e * BLOCK, (2 * e + 1) * BLOCK)
        edges.append((
            (tn(slopes[e][:, side], q[rows(b), :]) * SCALE).astype(BF16),
            tn(w_edge[rows(e), side], items[e][0]).astype(BF16),
        ))
    q_top[...] = nn(slopes[2], pair[2]) * SCALE
    pair_out[2] = (tn(slopes[2], qp[rows(6), :]) * SCALE).astype(BF16)
    pair_out[3] = tn(w_top[...], top_grad).astype(BF16)
    for i in range(2):
        pair_out[i] = jnp.where(odd, edges[0][i], edges[1][i])
        other_out[i] = jnp.where(odd, edges[1][i], edges[0][i])


def backward_inner_kernel(
    q, k, v, qp, kp, vp, w_mid, w_coarse, w_edge, g0, gc, off0, offc, sl_edge, q_edge, q_top, out,
    k_grad, v_grad, m0, m1, m2, m3,
    sl_mid, sl_coarse, buf, grads, q_grad,
):
    coarse = slopes_of([
        (gc[rows(c), :], vp[rows(c ^ 1), :], w_coarse[rows(c), :], offc[rows(c), :]) for c in range(6)
    ])
    for c, slope in enumerate(coarse):
        sl_coarse[rows(c), :] = slope
        grads[rows(c), :] = nn(slope, kp[rows(c ^ 1), :]) * SCALE
    inner = slopes_of([
        (g0[rows(b + 1), :], v[rows(b, 3), :], w_mid[rows(b), :], off0[rows(b + 1), :])
        for b in range(MID)
    ])
    for b, slope in enumerate(inner):
        sl_mid[rows(b), :] = slope
    e = grads[rows(4, 2), :] * 0.25 + spread(buf, q_top[...] * 0.125, 128)
    e = grads[rows(0, 4), :] * 0.5 + spread(buf, e, 256)
    spread(buf, e, 512)
    for b in range(GROUP):
        if b in (0, GROUP - 1):
            part = q_edge[rows(b // (GROUP - 1)), :]
        else:
            part = nn(inner[b - 1], k[rows(b - 1, 3), :]) * SCALE
        q_grad[rows(b), :] = (part + buf[rows(b), :]).astype(BF16)

    for at, message in zip(places(), (m0, m1, m2, m3)):
        message[0] = out[at, :]
        message[1] = q_grad[at, :]

    def key_value(factor, edge, mid, mid_c, right, right_c, res):
        for c in range(6):
            grads[rows(c ^ 1), :] = tn(mid_c[rows(c), :], right_c[rows(c), :])
        e = grads[rows(4, 2), :] * (0.25 * factor)
        e = grads[rows(0, 4), :] * (0.5 * factor) + spread(buf, e, 256)
        spread(buf, e, 512)
        for j in range(GROUP):
            total = None
            for side in range(3):
                b = j + 1 - side
                cols = pl.ds(side * BLOCK, BLOCK)
                if b in (0, GROUP - 1):
                    left = edge[rows(b // (GROUP - 1)), cols]
                elif 0 < b < GROUP - 1:
                    left = mid[rows(b - 1), cols]
                else:
                    continue
                part = tn(left, right[rows(b), :])
                total = part if total is None else total + part
            res[rows(j), :] = total * factor + buf[rows(j), :]

    key_value(SCALE, sl_edge, sl_mid, sl_coarse, q, qp, k_grad)
    key_value(1.0, w_edge, w_mid, w_coarse, g0, gc, v_grad)


def collect_kernel(k_grad, v_grad, pair, other, *refs):
    messages, buf = refs[:-1], refs[-1]
    odd = lax.rem(lax.axis_index("z"), 2) == 1
    for i, x in enumerate((k_grad, v_grad)):
        spread(buf, pair[2 + i].astype(F32) * 0.125, 128, 8)
        buf[...] += x[...]
        buf[rows(0), :] += jnp.where(odd, pair[i], other[i]).astype(F32)
        buf[rows(GROUP - 1), :] += jnp.where(odd, other[i], pair[i]).astype(F32)
        for at, message in zip(places(), messages):
            message[i] = buf[at, :].astype(BF16)


def regroup_kernel(*refs):
    parts, (own, away) = refs[:CHIPS], refs[CHIPS:]
    core, chip = lax.axis_index("c"), lax.axis_index("x")
    mine, theirs = at_block(core), at_block(1 - core)
    for step, part in zip(STEPS, parts):
        cols = pl.ds(pl.multiple_of((chip ^ step) * DH, DH), DH)
        for i in range(2):
            own[i, :, cols] = part[i, mine, :]
            away[i, :, cols] = part[i, theirs, :]


def finish_kernel(own, got, *refs):
    results, sem = refs[:-1], refs[-1]
    core = lax.axis_index("c")
    copies = []
    for i, x in enumerate(results):
        for j, (half, source) in enumerate(((1 - core, got), (core, own))):
            cols = pl.ds(pl.multiple_of(half * HALF, HALF), HALF)
            copies.append(pltpu.make_async_copy(source.at[i], x.at[:, cols], sem.at[j, i]))
    run_all(copies)


def swap_pair(x):
    return lax.ppermute(x, "z", [(i, i ^ 1) for i in range(lax.axis_size("z"))])


def swap_other(x):
    up = [(i, i + 1) for i in range(1, lax.axis_size("z") - 1, 2)]
    return lax.ppermute(x, "z", up + [(target, source) for source, target in up])


def swap_core(x):
    return lax.ppermute(x, "c", [(0, 1), (1, 0)])


def swap_chips(messages):
    return [messages[0]] + [
        lax.ppermute(message, "x", [(i, i ^ step) for i in range(CHIPS)])
        for step, message in zip(STEPS[1:], messages[1:])
    ]


def exchange(x, axes):
    return lax.all_to_all(x, axes, 0, 0, tiled=True)


def local(query, keys, values, gain, out_grad):
    token = ((BLOCK, query.shape[1]), BF16, HBM)
    part = ((2, 2 * BLOCK, DH), BF16)
    half = ((2, BLOCK, HALF), BF16)
    partners = GROUP * lax.axis_size("head")
    message = ((4, BLOCK, DH), BF16)
    edge = ((2, BLOCK, DH), BF16)
    whole = ((TOKENS, DH), BF16)
    whole_f = ((TOKENS, DH), F32)
    coarse = ((COARSE, DH), BF16)
    coarse_f = ((COARSE, DH), F32)
    one_f = ((BLOCK, DH), F32)
    two_f = ((2 * BLOCK, DH), F32)
    w_mids = ((MID * BLOCK, 3 * BLOCK), BF16)
    w_coarses = ((6 * BLOCK, BLOCK), BF16)
    w_edges = ((2 * BLOCK, 3 * BLOCK), BF16)
    w_tops = ((BLOCK, BLOCK), BF16)
    inner_f = (((MID + 6) * BLOCK, DH), F32)
    edge_sets = ((2, 3 * BLOCK, DH), BF16)
    shares = [((2, TOKENS >> level, DH), F32) for level in range(3)]
    features = query.shape[1] * lax.axis_size("head")

    head = lax.axis_index("c") * CHIPS + lax.axis_index("x")
    my_gain = lax.dynamic_slice_in_dim(gain, head * DH, DH).reshape(1, DH)

    def send(x, y):
        gots = [swap_core(one) for one in (x, y)]
        own = [lax.dynamic_slice_in_dim(one, lax.axis_index("c") * HALF, HALF, 1) for one in (x, y)]
        return swap_chips(call(pack_kernel, [part] * CHIPS, 4)(*own, *gots))

    got_keys = send(keys, values)
    got_queries = send(query, out_grad)
    k, v, kp, vp, pair, other = call(
        keys_kernel, [whole] * 2 + [coarse] * 2 + [message, edge], CHIPS, [whole_f]
    )(*got_keys)
    pair, other = swap_pair(pair), swap_other(other)
    q, d, qp = call(queries_kernel, [whole] * 2 + [coarse], CHIPS, [whole_f])(*got_queries)
    w_mid, w_coarse, *inner = call(
        forward_inner_kernel, [w_mids, w_coarses] + [inner_f] * 3, 6, flops=FLOPS
    )(q, k, v, qp, kp, vp)
    attn, stats, w_edge, w_top, share, share1, share2, edge_k, edge_v = call(
        forward_edge_kernel,
        [whole, ((partners, 2, GROUP, DH), F32), w_edges, w_tops] + shares + [edge_sets] * 2,
        11,
        [((3 * BLOCK, DH), F32)] * 3 + [whole_f] * 3,
    )(q, k, v, d, qp, pair, other, my_gain, *inner)
    stats = exchange(stats, ("x", "c", "head"))

    def backward_edge(*refs):
        backward_edge_kernel(features, *refs)

    out, pair_back, other_back, g0, gc, off0, offc, sl_edge, q_edge, q_top = call(
        backward_edge,
        [whole, message, edge, whole, coarse, whole_f, coarse_f, w_edges, two_f, one_f],
        14,
        [whole_f] * 2,
    )(stats, d, my_gain, attn, share, share1, share2, q, qp, pair, edge_k, edge_v, w_edge, w_top)
    pair_back, other_back = swap_pair(pair_back), swap_other(other_back)
    k_grad, v_grad, *messages = call(
        backward_inner_kernel,
        [whole_f, whole_f] + [part] * CHIPS,
        17,
        [w_mids, w_coarses, whole_f, coarse_f, whole],
        flops=2 * FLOPS,
    )(q, k, v, qp, kp, vp, w_mid, w_coarse, w_edge, g0, gc, off0, offc, sl_edge, q_edge, q_top, out)

    def deliver(messages):
        own, away = call(regroup_kernel, [half] * 2, CHIPS)(*swap_chips(messages))
        finish = call(finish_kernel, [token] * 2, 2, [pltpu.SemaphoreType.DMA((2, 2))])
        return finish(own, swap_core(away))

    out, q_grad = deliver(messages)
    messages = call(collect_kernel, [part] * CHIPS, 4, [whole_f])(k_grad, v_grad, pair_back, other_back)
    return (out, q_grad, *deliver(messages))


def solution(mesh):
    chips = (CHIPS, 2)
    axes = ("z", "x", "c", "head")
    heads = mesh.shape["head"]
    fine = Mesh(mesh.devices.reshape((mesh.shape["seq"] // GROUP, *chips, heads)), axes)
    spec = P(("z", "x", "c"), "head")
    in_specs = (spec, spec, spec, P("head"), spec)
    return jax.shard_map(
        local, mesh=fine, in_specs=in_specs, out_specs=(spec,) * 4, check_vma=False
    )
```

```python
import math

import jax
import jax.numpy as jnp
from jax import lax
from jax.experimental import pallas as pl
from jax.experimental.pallas import tpu as pltpu
from jax.sharding import Mesh, PartitionSpec as P

DH = 128
BLOCK = 128
GROUP = 8
CHIPS = 4
STEPS = (0, 2, 3, 1)
HALF = CHIPS * 128
MID = GROUP - 2
TOKENS = GROUP * BLOCK
COARSE = TOKENS // 2 + TOKENS // 4 + TOKENS // 8
START = {1: 0, 2: TOKENS // 2, 3: TOKENS // 2 + TOKENS // 4}
EPS = 1e-06
FLOOR = -1e30
FLOPS = 4 * 10**9
SCALE = 1.0 / math.sqrt(DH)
SHARP = SCALE * math.log2(math.e)
VMEM = pl.BlockSpec(memory_space=pltpu.VMEM)
HBM = pl.BlockSpec(memory_space=pltpu.HBM)
F32 = jnp.float32
BF16 = jnp.bfloat16


def call(kernel, outs, ins, scratch=(), flops=0, vmem=16):
    return pl.pallas_call(
        kernel,
        out_shape=[jax.ShapeDtypeStruct(*out[:2]) for out in outs],
        in_specs=[VMEM] * ins if isinstance(ins, int) else ins,
        out_specs=[out[2] if len(out) > 2 else VMEM for out in outs],
        scratch_shapes=[pltpu.VMEM(*one) if isinstance(one, tuple) else one for one in scratch],
        compiler_params=pltpu.CompilerParams(vmem_limit_bytes=vmem * 1024 * 1024),
        cost_estimate=pl.CostEstimate(flops=flops, bytes_accessed=0, transcendentals=0),
    )


def run_all(copies):
    for copy in copies:
        copy.start()
    for copy in copies:
        copy.wait()


def at_block(b):
    return pl.ds(pl.multiple_of(b * BLOCK, BLOCK), BLOCK)


def rows(b, n=1):
    return pl.ds(b * BLOCK, n * BLOCK)


def nt(a, b):
    return lax.dot_general(a, b, (((1,), (1,)), ((), ())), preferred_element_type=F32)


def nn(a, b):
    return lax.dot_general(a, b, (((1,), (0,)), ((), ())), preferred_element_type=F32)


def tn(a, b):
    return lax.dot_general(a, b, (((0,), (0,)), ((), ())), preferred_element_type=F32)


def pack_kernel(x, y, got_x, got_y, *messages):
    core, chip = lax.axis_index("c"), lax.axis_index("x")
    mine, theirs = at_block(core), at_block(1 - core)
    for step, message in zip(STEPS, messages):
        here = (chip ^ step) * DH
        cols = pl.ds(pl.multiple_of(core * HALF + here, DH), DH)
        for i, (own, got) in enumerate(((x, got_x), (y, got_y))):
            message[i, mine, :] = own[:, pl.ds(pl.multiple_of(here, DH), DH)]
            message[i, theirs, :] = got[:, cols]


def places():
    chip = lax.axis_index("x")
    return [pl.ds(pl.multiple_of((chip ^ step) * 2 * BLOCK, BLOCK), 2 * BLOCK) for step in STEPS]


def pool(x, p, f32):
    f32[...] = x[...].astype(F32)
    n = TOKENS
    for level in (1, 2, 3):
        n //= 2
        pooled = f32[pl.ds(0, n, 2), :] + f32[pl.ds(1, n, 2), :]
        p[pl.ds(START[level], n), :] = (pooled * 0.5**level).astype(BF16)
        f32[pl.ds(0, n), :] = pooled


def keys_kernel(*refs):
    parts, (k, v, kp, vp, pair, other, f32) = refs[:CHIPS], refs[CHIPS:]
    odd = lax.rem(lax.axis_index("z"), 2)
    for part, at in zip(parts, places()):
        k[at, :] = part[0]
        v[at, :] = part[1]
    pool(k, kp, f32)
    pool(v, vp, f32)
    near, far = at_block((1 - odd) * (GROUP - 1)), at_block(odd * (GROUP - 1))
    pair[0] = k[near, :]
    pair[1] = v[near, :]
    pair[2] = kp[pl.ds(START[3], BLOCK), :]
    pair[3] = vp[pl.ds(START[3], BLOCK), :]
    other[0] = k[far, :]
    other[1] = v[far, :]


def queries_kernel(*refs):
    parts, (q, d, qp, f32) = refs[:CHIPS], refs[CHIPS:]
    for part, at in zip(parts, places()):
        q[at, :] = part[0]
        d[at, :] = part[1]
    pool(q, qp, f32)


def spread(scratch, x, n, times=2):
    for j in range(times):
        scratch[pl.ds(j, n, times), :] = x
    return scratch[pl.ds(0, n * times), :]


def column(x):
    return jnp.sum(x, axis=1, keepdims=True)


def attend(items, tops, totals, sums):
    scores = []
    for queries, keys, _, _, invalid in items:
        one = nt(queries, keys)
        if invalid is not None:
            side, bad = invalid
            lane = lax.broadcasted_iota(jnp.int32, one.shape, 1) // BLOCK
            one = jnp.where((lane == side) & bad, FLOOR, one)
        scores.append(one)
    weights = []
    for one, (_, _, _, at, _) in zip(scores, items):
        top = jnp.max(one, axis=1, keepdims=True)
        tops[at, :] = jnp.broadcast_to(top, (BLOCK, DH))
        weights.append(jnp.exp2((one - top) * SHARP))
    rounded = [one.astype(BF16) for one in weights]
    for one, (_, _, values, at, _) in zip(rounded, items):
        both = nn(one, jnp.concatenate([values, jnp.ones_like(values)], axis=1))
        sums[at, :] = both[:, :DH]
        totals[at, :] = both[:, DH:]
    return rounded


def forward_inner_kernel(q, k, v, qp, kp, vp, w_mid, w_coarse, tops, totals, sums):
    inner = [
        (q[rows(b + 1), :], k[rows(b, 3), :], v[rows(b, 3), :], rows(b), None) for b in range(MID)
    ]
    for b, one in enumerate(attend(inner, tops, totals, sums)):
        w_mid[rows(b), :] = one
    coarse = [
        (qp[rows(c), :], kp[rows(c ^ 1), :], vp[rows(c ^ 1), :], rows(MID + c), None) for c in range(6)
    ]
    for c, one in enumerate(attend(coarse, tops, totals, sums)):
        w_coarse[rows(c), :] = one


def forward_edge_kernel(
    q, k, v, d, qp, pair, other, gain, tops, totals, sums,
    attn, stats, w_edge, w_top, share, share1, share2, edge_k, edge_v,
    e_tops, e_totals, e_sums, up_m, up_t, up_s,
):
    z = lax.axis_index("z")
    odd = lax.rem(z, 2) == 1
    for x, edge, i in ((k, edge_k, 0), (v, edge_v, 1)):
        edge[0, rows(0), :] = jnp.where(odd, pair[i], other[i])
        edge[0, rows(1, 2), :] = x[rows(0, 2), :]
        edge[1, rows(0, 2), :] = x[rows(GROUP - 2, 2), :]
        edge[1, rows(2), :] = jnp.where(odd, other[i], pair[i])
    last = z == lax.axis_size("z") - 1
    top3 = rows(2)
    items = [
        (q[rows(b), :], edge_k[e], edge_v[e], rows(e), invalid)
        for e, (b, invalid) in enumerate(((0, (0, z == 0)), (GROUP - 1, (2, last))))
    ]
    items.append((qp[rows(6), :], pair[2], pair[3], top3, None))
    w_edge[rows(0), :], w_edge[rows(1), :], w_top[...] = attend(items, e_tops, e_totals, e_sums)
    m, t, s = e_tops[top3, :], e_totals[top3, :] * 8.0, e_sums[top3, :] * 8.0
    n = TOKENS // 8
    for level, out in ((2, share2), (1, share1)):
        em, et, es = spread(up_m, m, n), spread(up_t, t, n), spread(up_s, s, n)
        n *= 2
        at = pl.ds(MID * BLOCK + START[level], n)
        own = tops[at, :]
        m = jnp.maximum(own, em)
        here = 2.0**level * jnp.exp2((own - m) * SHARP)
        up = jnp.exp2((em - m) * SHARP)
        t = here * totals[at, :] + up * et
        s = here * sums[at, :] + up * es
        out[0] = here
        out[1] = up
    spread(up_m, m, n), spread(up_t, t, n), spread(up_s, s, n)
    lane = lax.broadcasted_iota(jnp.int32, (BLOCK, DH), 1)
    columns = jnp.zeros((BLOCK, DH), F32)
    for b in range(GROUP):
        if b in (0, GROUP - 1):
            at, (mm, tt, ss) = rows(b // (GROUP - 1)), (e_tops, e_totals, e_sums)
        else:
            at, (mm, tt, ss) = rows(b - 1), (tops, totals, sums)
        own, em = mm[at, :], up_m[rows(b), :]
        m = jnp.maximum(own, em)
        here, up = jnp.exp2((own - m) * SHARP), jnp.exp2((em - m) * SHARP)
        inverse = 1.0 / (here * tt[at, :] + up * up_t[rows(b), :])
        here, up = here * inverse, up * inverse
        rounded = (here * ss[at, :] + up * up_s[rows(b), :]).astype(BF16)
        share[0, rows(b), :] = here
        share[1, rows(b), :] = up
        attn[rows(b), :] = rounded
        flat = rounded.astype(F32)
        scaled = d[rows(b), :].astype(F32) * gain[...]
        for i, one in enumerate((column(flat * flat), column(scaled * flat))):
            columns = jnp.where(lane == i * GROUP + b, one, columns)
    turned = columns.T[: 2 * GROUP].astype(BF16)
    stats[...] = jnp.broadcast_to(turned[None], stats.shape)


def slopes_of(items):
    pressures = [nt(grad, values) for grad, values, _, _ in items]
    slopes = []
    for pressure, (_, values, weights, offset) in zip(pressures, items):
        wide = jnp.concatenate([offset] * (values.shape[0] // BLOCK), axis=1)
        slopes.append((weights.astype(F32) * (pressure - wide)).astype(BF16))
    return slopes


def backward_edge_kernel(
    features,
    stats, d, gain, attn, share, share1, share2, q, qp, pair, edge_k, edge_v, w_edge, w_top,
    out, pair_out, other_out, g0, gc, off0, offc, sl_edge, q_edge, q_top,
    buf, buf2,
):
    odd = lax.rem(lax.axis_index("z"), 2) == 1
    sums = jnp.sum(stats[...].astype(F32), axis=0) * (1.0 / features)
    sums = sums.reshape(2, GROUP, BLOCK)
    inv_row = lax.rsqrt(sums[0] + EPS)
    drop_row = inv_row * inv_row * inv_row * sums[1]
    for b in range(GROUP):
        inv = jnp.broadcast_to(inv_row[b : b + 1], (BLOCK, DH)).T
        drop = jnp.broadcast_to(drop_row[b : b + 1], (BLOCK, DH)).T
        flat = attn[rows(b), :].astype(F32)
        out[rows(b), :] = (flat * (inv * gain[...])).astype(BF16)
        scaled = d[rows(b), :].astype(F32) * gain[...]
        grad = (inv * scaled - flat * drop).astype(BF16).astype(F32)
        dot = jnp.broadcast_to(column(grad * flat), (BLOCK, DH))
        here, up = share[0, rows(b), :], share[1, rows(b), :]
        g0[rows(b), :] = (here * grad).astype(BF16)
        off0[rows(b), :] = here * dot
        buf[rows(b), :] = up * grad
        buf2[rows(b), :] = up * dot
    n = TOKENS
    for level, sh in ((1, share1), (2, share2), (3, None)):
        n //= 2
        g = buf[pl.ds(0, n, 2), :] + buf[pl.ds(1, n, 2), :]
        o = buf2[pl.ds(0, n, 2), :] + buf2[pl.ds(1, n, 2), :]
        at = pl.ds(START[level], n)
        if sh is None:
            gc[at, :] = (g * 8.0).astype(BF16)
            offc[at, :] = o * 8.0
        else:
            here, up = sh[0], sh[1]
            gc[at, :] = (g * here).astype(BF16)
            offc[at, :] = o * here
            buf[pl.ds(0, n), :] = g * up
            buf2[pl.ds(0, n), :] = o * up
    items = [
        (g0[rows(b), :], edge_v[e], w_edge[rows(e), :], off0[rows(b), :])
        for e, b in ((0, 0), (1, GROUP - 1))
    ]
    top_grad = gc[rows(6), :]
    items.append((top_grad, pair[3], w_top[...], offc[rows(6), :]))
    slopes = slopes_of(items)
    edges = []
    for e, b in ((0, 0), (1, GROUP - 1)):
        sl_edge[rows(e), :] = slopes[e]
        q_edge[rows(e), :] = nn(slopes[e], edge_k[e]) * SCALE
        side = slice(2 * e * BLOCK, (2 * e + 1) * BLOCK)
        edges.append((
            (tn(slopes[e][:, side], q[rows(b), :]) * SCALE).astype(BF16),
            tn(w_edge[rows(e), side], items[e][0]).astype(BF16),
        ))
    q_top[...] = nn(slopes[2], pair[2]) * SCALE
    pair_out[2] = (tn(slopes[2], qp[rows(6), :]) * SCALE).astype(BF16)
    pair_out[3] = tn(w_top[...], top_grad).astype(BF16)
    for i in range(2):
        pair_out[i] = jnp.where(odd, edges[0][i], edges[1][i])
        other_out[i] = jnp.where(odd, edges[1][i], edges[0][i])


def backward_inner_kernel(
    q, k, v, qp, kp, vp, w_mid, w_coarse, w_edge, g0, gc, off0, offc, sl_edge, q_edge, q_top, out,
    pair, other, k_grad, v_grad, m0, m1, m2, m3, pair_out, other_out,
    sl_mid, sl_coarse, buf, grads, q_grad,
):
    coarse = slopes_of([
        (gc[rows(c), :], vp[rows(c ^ 1), :], w_coarse[rows(c), :], offc[rows(c), :]) for c in range(6)
    ])
    for c, slope in enumerate(coarse):
        sl_coarse[rows(c), :] = slope
        grads[rows(c), :] = nn(slope, kp[rows(c ^ 1), :]) * SCALE
    inner = slopes_of([
        (g0[rows(b + 1), :], v[rows(b, 3), :], w_mid[rows(b), :], off0[rows(b + 1), :])
        for b in range(MID)
    ])
    for b, slope in enumerate(inner):
        sl_mid[rows(b), :] = slope
    e = grads[rows(4, 2), :] * 0.25 + spread(buf, q_top[...] * 0.125, 128)
    e = grads[rows(0, 4), :] * 0.5 + spread(buf, e, 256)
    spread(buf, e, 512)
    for b in range(GROUP):
        if b in (0, GROUP - 1):
            part = q_edge[rows(b // (GROUP - 1)), :]
        else:
            part = nn(inner[b - 1], k[rows(b - 1, 3), :]) * SCALE
        q_grad[rows(b), :] = (part + buf[rows(b), :]).astype(BF16)

    pair_out[...] = pair[...]
    other_out[...] = other[...]
    for at, message in zip(places(), (m0, m1, m2, m3)):
        message[0] = out[at, :]
        message[1] = q_grad[at, :]

    def key_value(factor, edge, mid, mid_c, right, right_c, res):
        for c in range(6):
            grads[rows(c ^ 1), :] = tn(mid_c[rows(c), :], right_c[rows(c), :])
        e = grads[rows(4, 2), :] * (0.25 * factor)
        e = grads[rows(0, 4), :] * (0.5 * factor) + spread(buf, e, 256)
        spread(buf, e, 512)
        for j in range(GROUP):
            total = None
            for side in range(3):
                b = j + 1 - side
                cols = pl.ds(side * BLOCK, BLOCK)
                if b in (0, GROUP - 1):
                    left = edge[rows(b // (GROUP - 1)), cols]
                elif 0 < b < GROUP - 1:
                    left = mid[rows(b - 1), cols]
                else:
                    continue
                part = tn(left, right[rows(b), :])
                total = part if total is None else total + part
            res[rows(j), :] = total * factor + buf[rows(j), :]

    key_value(SCALE, sl_edge, sl_mid, sl_coarse, q, qp, k_grad)
    key_value(1.0, w_edge, w_mid, w_coarse, g0, gc, v_grad)


def collect_kernel(k_grad, v_grad, pair, other, *refs):
    messages, buf = refs[:-1], refs[-1]
    odd = lax.rem(lax.axis_index("z"), 2) == 1
    for i, x in enumerate((k_grad, v_grad)):
        spread(buf, pair[2 + i].astype(F32) * 0.125, 128, 8)
        buf[...] += x[...]
        buf[rows(0), :] += jnp.where(odd, pair[i], other[i]).astype(F32)
        buf[rows(GROUP - 1), :] += jnp.where(odd, other[i], pair[i]).astype(F32)
        for at, message in zip(places(), messages):
            message[i] = buf[at, :].astype(BF16)


def regroup_kernel(*refs):
    parts, (own, away) = refs[:CHIPS], refs[CHIPS:]
    core, chip = lax.axis_index("c"), lax.axis_index("x")
    mine, theirs = at_block(core), at_block(1 - core)
    for step, part in zip(STEPS, parts):
        cols = pl.ds(pl.multiple_of((chip ^ step) * DH, DH), DH)
        for i in range(2):
            own[i, :, cols] = part[i, mine, :]
            away[i, :, cols] = part[i, theirs, :]


def finish_kernel(own, got, *refs):
    results, sem = refs[:-1], refs[-1]
    core = lax.axis_index("c")
    copies = []
    for i, x in enumerate(results):
        for j, (half, source) in enumerate(((1 - core, got), (core, own))):
            cols = pl.ds(pl.multiple_of(half * HALF, HALF), HALF)
            copies.append(pltpu.make_async_copy(source.at[i], x.at[:, cols], sem.at[j, i]))
    run_all(copies)


def swap_pair(x):
    return lax.ppermute(x, "z", [(i, i ^ 1) for i in range(lax.axis_size("z"))])


def swap_other(x):
    up = [(i, i + 1) for i in range(1, lax.axis_size("z") - 1, 2)]
    return lax.ppermute(x, "z", up + [(target, source) for source, target in up])


def swap_core(x):
    return lax.ppermute(x, "c", [(0, 1), (1, 0)])


def swap_chips(messages):
    return [messages[0]] + [
        lax.ppermute(message, "x", [(i, i ^ step) for i in range(CHIPS)])
        for step, message in zip(STEPS[1:], messages[1:])
    ]


def exchange(x, axes):
    return lax.all_to_all(x, axes, 0, 0, tiled=True)


def local(query, keys, values, gain, out_grad):
    token = ((BLOCK, query.shape[1]), BF16, HBM)
    part = ((2, 2 * BLOCK, DH), BF16)
    half = ((2, BLOCK, HALF), BF16)
    partners = GROUP * lax.axis_size("head")
    message = ((4, BLOCK, DH), BF16)
    edge = ((2, BLOCK, DH), BF16)
    whole = ((TOKENS, DH), BF16)
    whole_f = ((TOKENS, DH), F32)
    coarse = ((COARSE, DH), BF16)
    coarse_f = ((COARSE, DH), F32)
    one_f = ((BLOCK, DH), F32)
    two_f = ((2 * BLOCK, DH), F32)
    w_mids = ((MID * BLOCK, 3 * BLOCK), BF16)
    w_coarses = ((6 * BLOCK, BLOCK), BF16)
    w_edges = ((2 * BLOCK, 3 * BLOCK), BF16)
    w_tops = ((BLOCK, BLOCK), BF16)
    inner_f = (((MID + 6) * BLOCK, DH), F32)
    edge_sets = ((2, 3 * BLOCK, DH), BF16)
    shares = [((2, TOKENS >> level, DH), F32) for level in range(3)]
    features = query.shape[1] * lax.axis_size("head")

    head = lax.axis_index("c") * CHIPS + lax.axis_index("x")
    my_gain = lax.dynamic_slice_in_dim(gain, head * DH, DH).reshape(1, DH)

    def send(x, y):
        gots = [swap_core(one) for one in (x, y)]
        own = [lax.dynamic_slice_in_dim(one, lax.axis_index("c") * HALF, HALF, 1) for one in (x, y)]
        return swap_chips(call(pack_kernel, [part] * CHIPS, 4)(*own, *gots))

    got_keys = send(keys, values)
    got_queries = send(query, out_grad)
    k, v, kp, vp, pair, other = call(
        keys_kernel, [whole] * 2 + [coarse] * 2 + [message, edge], CHIPS, [whole_f]
    )(*got_keys)
    pair, other = swap_pair(pair), swap_other(other)
    q, d, qp = call(queries_kernel, [whole] * 2 + [coarse], CHIPS, [whole_f])(*got_queries)
    w_mid, w_coarse, *inner = call(
        forward_inner_kernel, [w_mids, w_coarses] + [inner_f] * 3, 6, flops=FLOPS
    )(q, k, v, qp, kp, vp)
    attn, stats, w_edge, w_top, share, share1, share2, edge_k, edge_v = call(
        forward_edge_kernel,
        [whole, ((partners, 2 * GROUP, DH), BF16), w_edges, w_tops] + shares + [edge_sets] * 2,
        11,
        [((3 * BLOCK, DH), F32)] * 3 + [whole_f] * 3,
    )(q, k, v, d, qp, pair, other, my_gain, *inner)
    stats = exchange(stats, ("x", "c", "head"))

    def backward_edge(*refs):
        backward_edge_kernel(features, *refs)

    out, pair_back, other_back, g0, gc, off0, offc, sl_edge, q_edge, q_top = call(
        backward_edge,
        [whole, message, edge, whole, coarse, whole_f, coarse_f, w_edges, two_f, one_f],
        14,
        [whole_f] * 2,
    )(stats, d, my_gain, attn, share, share1, share2, q, qp, pair, edge_k, edge_v, w_edge, w_top)
    k_grad, v_grad, *messages, pair_back, other_back = call(
        backward_inner_kernel,
        [whole_f, whole_f] + [part] * CHIPS + [message, edge],
        19,
        [w_mids, w_coarses, whole_f, coarse_f, whole],
        flops=2 * FLOPS,
    )(q, k, v, qp, kp, vp, w_mid, w_coarse, w_edge, g0, gc, off0, offc, sl_edge, q_edge, q_top, out,
      pair_back, other_back)
    pair_back, other_back = swap_pair(pair_back), swap_other(other_back)

    def deliver(messages):
        own, away = call(regroup_kernel, [half] * 2, CHIPS)(*swap_chips(messages))
        finish = call(finish_kernel, [token] * 2, 2, [pltpu.SemaphoreType.DMA((2, 2))])
        return finish(own, swap_core(away))

    out, q_grad = deliver(messages)
    messages = call(collect_kernel, [part] * CHIPS, 4, [whole_f])(k_grad, v_grad, pair_back, other_back)
    return (out, q_grad, *deliver(messages))


def solution(mesh):
    chips = (CHIPS, 2)
    axes = ("z", "x", "c", "head")
    heads = mesh.shape["head"]
    fine = Mesh(mesh.devices.reshape((mesh.shape["seq"] // GROUP, *chips, heads)), axes)
    spec = P(("z", "x", "c"), "head")
    in_specs = (spec, spec, spec, P("head"), spec)
    return jax.shard_map(
        local, mesh=fine, in_specs=in_specs, out_specs=(spec,) * 4, check_vma=False
    )
```

```python
import math

import jax
import jax.numpy as jnp
from jax import lax
from jax.experimental import pallas as pl
from jax.experimental.pallas import tpu as pltpu
from jax.sharding import Mesh, PartitionSpec as P

DH = 128
BLOCK = 128
GROUP = 8
CHIPS = 4
STEPS = (0, 2, 3, 1)
HALF = CHIPS * 128
MID = GROUP - 2
TOKENS = GROUP * BLOCK
COARSE = TOKENS // 2 + TOKENS // 4 + TOKENS // 8
START = {1: 0, 2: TOKENS // 2, 3: TOKENS // 2 + TOKENS // 4}
EPS = 1e-06
FLOOR = -1e30
FLOPS = 10**8
SCALE = 1.0 / math.sqrt(DH)
SHARP = SCALE * math.log2(math.e)
VMEM = pl.BlockSpec(memory_space=pltpu.VMEM)
HBM = pl.BlockSpec(memory_space=pltpu.HBM)
F32 = jnp.float32
BF16 = jnp.bfloat16


def call(kernel, outs, ins, scratch=(), flops=0, vmem=16):
    return pl.pallas_call(
        kernel,
        out_shape=[jax.ShapeDtypeStruct(*out[:2]) for out in outs],
        in_specs=[VMEM] * ins if isinstance(ins, int) else ins,
        out_specs=[out[2] if len(out) > 2 else VMEM for out in outs],
        scratch_shapes=[pltpu.VMEM(*one) if isinstance(one, tuple) else one for one in scratch],
        compiler_params=pltpu.CompilerParams(vmem_limit_bytes=vmem * 1024 * 1024),
        cost_estimate=pl.CostEstimate(flops=flops, bytes_accessed=0, transcendentals=0),
    )


def run_all(copies):
    for copy in copies:
        copy.start()
    for copy in copies:
        copy.wait()


def at_block(b):
    return pl.ds(pl.multiple_of(b * BLOCK, BLOCK), BLOCK)


def rows(b, n=1):
    return pl.ds(b * BLOCK, n * BLOCK)


def nt(a, b):
    return lax.dot_general(a, b, (((1,), (1,)), ((), ())), preferred_element_type=F32)


def nn(a, b):
    return lax.dot_general(a, b, (((1,), (0,)), ((), ())), preferred_element_type=F32)


def tn(a, b):
    return lax.dot_general(a, b, (((0,), (0,)), ((), ())), preferred_element_type=F32)


def pack_kernel(x, y, got_x, got_y, *messages):
    core, chip = lax.axis_index("c"), lax.axis_index("x")
    mine, theirs = at_block(core), at_block(1 - core)
    for step, message in zip(STEPS, messages):
        here = (chip ^ step) * DH
        cols = pl.ds(pl.multiple_of(core * HALF + here, DH), DH)
        for i, (own, got) in enumerate(((x, got_x), (y, got_y))):
            message[i, mine, :] = own[:, pl.ds(pl.multiple_of(here, DH), DH)]
            message[i, theirs, :] = got[:, cols]


def places():
    chip = lax.axis_index("x")
    return [pl.ds(pl.multiple_of((chip ^ step) * 2 * BLOCK, BLOCK), 2 * BLOCK) for step in STEPS]


def pool(x, p, f32):
    f32[...] = x[...].astype(F32)
    n = TOKENS
    for level in (1, 2, 3):
        n //= 2
        pooled = f32[pl.ds(0, n, 2), :] + f32[pl.ds(1, n, 2), :]
        p[pl.ds(START[level], n), :] = (pooled * 0.5**level).astype(BF16)
        f32[pl.ds(0, n), :] = pooled


def keys_kernel(*refs):
    parts, (k, v, kp, vp, pair, other, f32) = refs[:CHIPS], refs[CHIPS:]
    odd = lax.rem(lax.axis_index("z"), 2)
    for part, at in zip(parts, places()):
        k[at, :] = part[0]
        v[at, :] = part[1]
    pool(k, kp, f32)
    pool(v, vp, f32)
    near, far = at_block((1 - odd) * (GROUP - 1)), at_block(odd * (GROUP - 1))
    pair[0] = k[near, :]
    pair[1] = v[near, :]
    pair[2] = kp[pl.ds(START[3], BLOCK), :]
    pair[3] = vp[pl.ds(START[3], BLOCK), :]
    other[0] = k[far, :]
    other[1] = v[far, :]


def queries_kernel(*refs):
    parts, (q, d, qp, f32) = refs[:CHIPS], refs[CHIPS:]
    for part, at in zip(parts, places()):
        q[at, :] = part[0]
        d[at, :] = part[1]
    pool(q, qp, f32)


def spread(scratch, x, n, times=2):
    for j in range(times):
        scratch[pl.ds(j, n, times), :] = x
    return scratch[pl.ds(0, n * times), :]


def column(x):
    return jnp.sum(x, axis=1, keepdims=True)


def attend(items, tops, totals, sums):
    scores = []
    for queries, keys, _, _, invalid in items:
        one = nt(queries, keys)
        if invalid is not None:
            side, bad = invalid
            lane = lax.broadcasted_iota(jnp.int32, one.shape, 1) // BLOCK
            one = jnp.where((lane == side) & bad, FLOOR, one)
        scores.append(one)
    weights = []
    for one, (_, _, _, at, _) in zip(scores, items):
        top = jnp.max(one, axis=1, keepdims=True)
        tops[at, :] = jnp.broadcast_to(top, (BLOCK, DH))
        weights.append(jnp.exp2((one - top) * SHARP))
    rounded = [one.astype(BF16) for one in weights]
    for one, (_, _, values, at, _) in zip(rounded, items):
        both = nn(one, jnp.concatenate([values, jnp.ones_like(values)], axis=1))
        sums[at, :] = both[:, :DH]
        totals[at, :] = both[:, DH:]
    return rounded


def forward_inner_kernel(q, k, v, qp, kp, vp, w_mid, w_coarse, tops, totals, sums):
    inner = [
        (q[rows(b + 1), :], k[rows(b, 3), :], v[rows(b, 3), :], rows(b), None) for b in range(MID)
    ]
    for b, one in enumerate(attend(inner, tops, totals, sums)):
        w_mid[rows(b), :] = one
    coarse = [
        (qp[rows(c), :], kp[rows(c ^ 1), :], vp[rows(c ^ 1), :], rows(MID + c), None) for c in range(6)
    ]
    for c, one in enumerate(attend(coarse, tops, totals, sums)):
        w_coarse[rows(c), :] = one


def forward_edge_kernel(
    q, k, v, d, qp, pair, other, gain, tops, totals, sums,
    attn, stats, w_edge, w_top, share, share1, share2, edge_k, edge_v,
    e_tops, e_totals, e_sums, up_m, up_t, up_s,
):
    z = lax.axis_index("z")
    odd = lax.rem(z, 2) == 1
    for x, edge, i in ((k, edge_k, 0), (v, edge_v, 1)):
        edge[0, rows(0), :] = jnp.where(odd, pair[i], other[i])
        edge[0, rows(1, 2), :] = x[rows(0, 2), :]
        edge[1, rows(0, 2), :] = x[rows(GROUP - 2, 2), :]
        edge[1, rows(2), :] = jnp.where(odd, other[i], pair[i])
    last = z == lax.axis_size("z") - 1
    top3 = rows(2)
    items = [
        (q[rows(b), :], edge_k[e], edge_v[e], rows(e), invalid)
        for e, (b, invalid) in enumerate(((0, (0, z == 0)), (GROUP - 1, (2, last))))
    ]
    items.append((qp[rows(6), :], pair[2], pair[3], top3, None))
    w_edge[rows(0), :], w_edge[rows(1), :], w_top[...] = attend(items, e_tops, e_totals, e_sums)
    m, t, s = e_tops[top3, :], e_totals[top3, :] * 8.0, e_sums[top3, :] * 8.0
    n = TOKENS // 8
    for level, out in ((2, share2), (1, share1)):
        em, et, es = spread(up_m, m, n), spread(up_t, t, n), spread(up_s, s, n)
        n *= 2
        at = pl.ds(MID * BLOCK + START[level], n)
        own = tops[at, :]
        m = jnp.maximum(own, em)
        here = 2.0**level * jnp.exp2((own - m) * SHARP)
        up = jnp.exp2((em - m) * SHARP)
        t = here * totals[at, :] + up * et
        s = here * sums[at, :] + up * es
        out[0] = here
        out[1] = up
    spread(up_m, m, n), spread(up_t, t, n), spread(up_s, s, n)
    lane = lax.broadcasted_iota(jnp.int32, (BLOCK, DH), 1)
    columns = jnp.zeros((BLOCK, DH), F32)
    for b in range(GROUP):
        if b in (0, GROUP - 1):
            at, (mm, tt, ss) = rows(b // (GROUP - 1)), (e_tops, e_totals, e_sums)
        else:
            at, (mm, tt, ss) = rows(b - 1), (tops, totals, sums)
        own, em = mm[at, :], up_m[rows(b), :]
        m = jnp.maximum(own, em)
        here, up = jnp.exp2((own - m) * SHARP), jnp.exp2((em - m) * SHARP)
        inverse = 1.0 / (here * tt[at, :] + up * up_t[rows(b), :])
        here, up = here * inverse, up * inverse
        rounded = (here * ss[at, :] + up * up_s[rows(b), :]).astype(BF16)
        share[0, rows(b), :] = here
        share[1, rows(b), :] = up
        attn[rows(b), :] = rounded
        flat = rounded.astype(F32)
        scaled = d[rows(b), :].astype(F32) * gain[...]
        for i, one in enumerate((column(flat * flat), column(scaled * flat))):
            columns = jnp.where(lane == i * GROUP + b, one, columns)
    turned = columns.T[: 2 * GROUP].astype(BF16)
    stats[...] = jnp.broadcast_to(turned[None], stats.shape)


def slopes_of(items):
    pressures = [nt(grad, values) for grad, values, _, _ in items]
    slopes = []
    for pressure, (_, values, weights, offset) in zip(pressures, items):
        wide = jnp.concatenate([offset] * (values.shape[0] // BLOCK), axis=1)
        slopes.append((weights.astype(F32) * (pressure - wide)).astype(BF16))
    return slopes


def backward_edge_kernel(
    features,
    stats, d, gain, attn, share, share1, share2, q, qp, pair, edge_k, edge_v, w_edge, w_top,
    out, pair_out, other_out, g0, gc, off0, offc, sl_edge, q_edge, q_top,
    buf, buf2,
):
    odd = lax.rem(lax.axis_index("z"), 2) == 1
    sums = jnp.sum(stats[...].astype(F32), axis=0) * (1.0 / features)
    sums = sums.reshape(2, GROUP, BLOCK)
    inv_row = lax.rsqrt(sums[0] + EPS)
    drop_row = inv_row * inv_row * inv_row * sums[1]
    for b in range(GROUP):
        inv = jnp.broadcast_to(inv_row[b : b + 1], (BLOCK, DH)).T
        drop = jnp.broadcast_to(drop_row[b : b + 1], (BLOCK, DH)).T
        flat = attn[rows(b), :].astype(F32)
        out[rows(b), :] = (flat * (inv * gain[...])).astype(BF16)
        scaled = d[rows(b), :].astype(F32) * gain[...]
        grad = (inv * scaled - flat * drop).astype(BF16).astype(F32)
        dot = jnp.broadcast_to(column(grad * flat), (BLOCK, DH))
        here, up = share[0, rows(b), :], share[1, rows(b), :]
        g0[rows(b), :] = (here * grad).astype(BF16)
        off0[rows(b), :] = here * dot
        buf[rows(b), :] = up * grad
        buf2[rows(b), :] = up * dot
    n = TOKENS
    for level, sh in ((1, share1), (2, share2), (3, None)):
        n //= 2
        g = buf[pl.ds(0, n, 2), :] + buf[pl.ds(1, n, 2), :]
        o = buf2[pl.ds(0, n, 2), :] + buf2[pl.ds(1, n, 2), :]
        at = pl.ds(START[level], n)
        if sh is None:
            gc[at, :] = (g * 8.0).astype(BF16)
            offc[at, :] = o * 8.0
        else:
            here, up = sh[0], sh[1]
            gc[at, :] = (g * here).astype(BF16)
            offc[at, :] = o * here
            buf[pl.ds(0, n), :] = g * up
            buf2[pl.ds(0, n), :] = o * up
    items = [
        (g0[rows(b), :], edge_v[e], w_edge[rows(e), :], off0[rows(b), :])
        for e, b in ((0, 0), (1, GROUP - 1))
    ]
    top_grad = gc[rows(6), :]
    items.append((top_grad, pair[3], w_top[...], offc[rows(6), :]))
    slopes = slopes_of(items)
    edges = []
    for e, b in ((0, 0), (1, GROUP - 1)):
        sl_edge[rows(e), :] = slopes[e]
        q_edge[rows(e), :] = nn(slopes[e], edge_k[e]) * SCALE
        side = slice(2 * e * BLOCK, (2 * e + 1) * BLOCK)
        edges.append((
            (tn(slopes[e][:, side], q[rows(b), :]) * SCALE).astype(BF16),
            tn(w_edge[rows(e), side], items[e][0]).astype(BF16),
        ))
    q_top[...] = nn(slopes[2], pair[2]) * SCALE
    pair_out[2] = (tn(slopes[2], qp[rows(6), :]) * SCALE).astype(BF16)
    pair_out[3] = tn(w_top[...], top_grad).astype(BF16)
    for i in range(2):
        pair_out[i] = jnp.where(odd, edges[0][i], edges[1][i])
        other_out[i] = jnp.where(odd, edges[1][i], edges[0][i])


def backward_inner_kernel(
    q, k, v, qp, kp, vp, w_mid, w_coarse, w_edge, g0, gc, off0, offc, sl_edge, q_edge, q_top, out,
    pair, other, k_grad, v_grad, m0, m1, m2, m3, pair_out, other_out,
    sl_mid, sl_coarse, buf, grads, q_grad,
):
    coarse = slopes_of([
        (gc[rows(c), :], vp[rows(c ^ 1), :], w_coarse[rows(c), :], offc[rows(c), :]) for c in range(6)
    ])
    for c, slope in enumerate(coarse):
        sl_coarse[rows(c), :] = slope
        grads[rows(c), :] = nn(slope, kp[rows(c ^ 1), :]) * SCALE
    inner = slopes_of([
        (g0[rows(b + 1), :], v[rows(b, 3), :], w_mid[rows(b), :], off0[rows(b + 1), :])
        for b in range(MID)
    ])
    for b, slope in enumerate(inner):
        sl_mid[rows(b), :] = slope
    e = grads[rows(4, 2), :] * 0.25 + spread(buf, q_top[...] * 0.125, 128)
    e = grads[rows(0, 4), :] * 0.5 + spread(buf, e, 256)
    spread(buf, e, 512)
    for b in range(GROUP):
        if b in (0, GROUP - 1):
            part = q_edge[rows(b // (GROUP - 1)), :]
        else:
            part = nn(inner[b - 1], k[rows(b - 1, 3), :]) * SCALE
        q_grad[rows(b), :] = (part + buf[rows(b), :]).astype(BF16)

    pair_out[...] = pair[...]
    other_out[...] = other[...]
    for at, message in zip(places(), (m0, m1, m2, m3)):
        message[0] = out[at, :]
        message[1] = q_grad[at, :]

    def key_value(factor, edge, mid, mid_c, right, right_c, res):
        for c in range(6):
            grads[rows(c ^ 1), :] = tn(mid_c[rows(c), :], right_c[rows(c), :])
        e = grads[rows(4, 2), :] * (0.25 * factor)
        e = grads[rows(0, 4), :] * (0.5 * factor) + spread(buf, e, 256)
        spread(buf, e, 512)
        for j in range(GROUP):
            total = None
            for side in range(3):
                b = j + 1 - side
                cols = pl.ds(side * BLOCK, BLOCK)
                if b in (0, GROUP - 1):
                    left = edge[rows(b // (GROUP - 1)), cols]
                elif 0 < b < GROUP - 1:
                    left = mid[rows(b - 1), cols]
                else:
                    continue
                part = tn(left, right[rows(b), :])
                total = part if total is None else total + part
            res[rows(j), :] = total * factor + buf[rows(j), :]

    key_value(SCALE, sl_edge, sl_mid, sl_coarse, q, qp, k_grad)
    key_value(1.0, w_edge, w_mid, w_coarse, g0, gc, v_grad)


def collect_kernel(k_grad, v_grad, pair, other, *refs):
    messages, buf = refs[:-1], refs[-1]
    odd = lax.rem(lax.axis_index("z"), 2) == 1
    for i, x in enumerate((k_grad, v_grad)):
        spread(buf, pair[2 + i].astype(F32) * 0.125, 128, 8)
        buf[...] += x[...]
        buf[rows(0), :] += jnp.where(odd, pair[i], other[i]).astype(F32)
        buf[rows(GROUP - 1), :] += jnp.where(odd, other[i], pair[i]).astype(F32)
        for at, message in zip(places(), messages):
            message[i] = buf[at, :].astype(BF16)


def regroup_kernel(*refs):
    parts, (own, away) = refs[:CHIPS], refs[CHIPS:]
    core, chip = lax.axis_index("c"), lax.axis_index("x")
    mine, theirs = at_block(core), at_block(1 - core)
    for step, part in zip(STEPS, parts):
        cols = pl.ds(pl.multiple_of((chip ^ step) * DH, DH), DH)
        for i in range(2):
            own[i, :, cols] = part[i, mine, :]
            away[i, :, cols] = part[i, theirs, :]


def finish_kernel(own, got, *refs):
    results, sem = refs[:-1], refs[-1]
    core = lax.axis_index("c")
    copies = []
    for i, x in enumerate(results):
        for j, (half, source) in enumerate(((1 - core, got), (core, own))):
            cols = pl.ds(pl.multiple_of(half * HALF, HALF), HALF)
            copies.append(pltpu.make_async_copy(source.at[i], x.at[:, cols], sem.at[j, i]))
    run_all(copies)


def swap_pair(x):
    return lax.ppermute(x, "z", [(i, i ^ 1) for i in range(lax.axis_size("z"))])


def swap_other(x):
    up = [(i, i + 1) for i in range(1, lax.axis_size("z") - 1, 2)]
    return lax.ppermute(x, "z", up + [(target, source) for source, target in up])


def swap_core(x):
    return lax.ppermute(x, "c", [(0, 1), (1, 0)])


def swap_chips(messages):
    return [messages[0]] + [
        lax.ppermute(message, "x", [(i, i ^ step) for i in range(CHIPS)])
        for step, message in zip(STEPS[1:], messages[1:])
    ]


def exchange(x, axes):
    return lax.all_to_all(x, axes, 0, 0, tiled=True)


def local(query, keys, values, gain, out_grad):
    token = ((BLOCK, query.shape[1]), BF16, HBM)
    part = ((2, 2 * BLOCK, DH), BF16)
    half = ((2, BLOCK, HALF), BF16)
    partners = GROUP * lax.axis_size("head")
    message = ((4, BLOCK, DH), BF16)
    edge = ((2, BLOCK, DH), BF16)
    whole = ((TOKENS, DH), BF16)
    whole_f = ((TOKENS, DH), F32)
    coarse = ((COARSE, DH), BF16)
    coarse_f = ((COARSE, DH), F32)
    one_f = ((BLOCK, DH), F32)
    two_f = ((2 * BLOCK, DH), F32)
    w_mids = ((MID * BLOCK, 3 * BLOCK), BF16)
    w_coarses = ((6 * BLOCK, BLOCK), BF16)
    w_edges = ((2 * BLOCK, 3 * BLOCK), BF16)
    w_tops = ((BLOCK, BLOCK), BF16)
    inner_f = (((MID + 6) * BLOCK, DH), F32)
    edge_sets = ((2, 3 * BLOCK, DH), BF16)
    shares = [((2, TOKENS >> level, DH), F32) for level in range(3)]
    features = query.shape[1] * lax.axis_size("head")

    head = lax.axis_index("c") * CHIPS + lax.axis_index("x")
    my_gain = lax.dynamic_slice_in_dim(gain, head * DH, DH).reshape(1, DH)

    def send(x, y):
        gots = [swap_core(one) for one in (x, y)]
        own = [lax.dynamic_slice_in_dim(one, lax.axis_index("c") * HALF, HALF, 1) for one in (x, y)]
        return swap_chips(call(pack_kernel, [part] * CHIPS, 4)(*own, *gots))

    got_keys = send(keys, values)
    got_queries = send(query, out_grad)
    k, v, kp, vp, pair, other = call(
        keys_kernel, [whole] * 2 + [coarse] * 2 + [message, edge], CHIPS, [whole_f]
    )(*got_keys)
    pair, other = swap_pair(pair), swap_other(other)
    q, d, qp = call(queries_kernel, [whole] * 2 + [coarse], CHIPS, [whole_f])(*got_queries)
    w_mid, w_coarse, *inner = call(
        forward_inner_kernel, [w_mids, w_coarses] + [inner_f] * 3, 6, flops=FLOPS
    )(q, k, v, qp, kp, vp)
    attn, stats, w_edge, w_top, share, share1, share2, edge_k, edge_v = call(
        forward_edge_kernel,
        [whole, ((partners, 2 * GROUP, DH), BF16), w_edges, w_tops] + shares + [edge_sets] * 2,
        11,
        [((3 * BLOCK, DH), F32)] * 3 + [whole_f] * 3,
    )(q, k, v, d, qp, pair, other, my_gain, *inner)
    stats = exchange(stats, ("x", "c", "head"))

    def backward_edge(*refs):
        backward_edge_kernel(features, *refs)

    out, pair_back, other_back, g0, gc, off0, offc, sl_edge, q_edge, q_top = call(
        backward_edge,
        [whole, message, edge, whole, coarse, whole_f, coarse_f, w_edges, two_f, one_f],
        14,
        [whole_f] * 2,
    )(stats, d, my_gain, attn, share, share1, share2, q, qp, pair, edge_k, edge_v, w_edge, w_top)
    k_grad, v_grad, *messages, pair_back, other_back = call(
        backward_inner_kernel,
        [whole_f, whole_f] + [part] * CHIPS + [message, edge],
        19,
        [w_mids, w_coarses, whole_f, coarse_f, whole],
        flops=2 * FLOPS,
    )(q, k, v, qp, kp, vp, w_mid, w_coarse, w_edge, g0, gc, off0, offc, sl_edge, q_edge, q_top, out,
      pair_back, other_back)
    pair_back, other_back = swap_pair(pair_back), swap_other(other_back)

    def deliver(messages):
        own, away = call(regroup_kernel, [half] * 2, CHIPS)(*swap_chips(messages))
        finish = call(finish_kernel, [token] * 2, 2, [pltpu.SemaphoreType.DMA((2, 2))])
        return finish(own, swap_core(away))

    out, q_grad = deliver(messages)
    messages = call(collect_kernel, [part] * CHIPS, 4, [whole_f])(k_grad, v_grad, pair_back, other_back)
    return (out, q_grad, *deliver(messages))


def solution(mesh):
    chips = (CHIPS, 2)
    axes = ("z", "x", "c", "head")
    heads = mesh.shape["head"]
    fine = Mesh(mesh.devices.reshape((mesh.shape["seq"] // GROUP, *chips, heads)), axes)
    spec = P(("z", "x", "c"), "head")
    in_specs = (spec, spec, spec, P("head"), spec)
    return jax.shard_map(
        local, mesh=fine, in_specs=in_specs, out_specs=(spec,) * 4, check_vma=False
    )
```

```python
import math

import jax
import jax.numpy as jnp
from jax import lax
from jax.experimental import pallas as pl
from jax.experimental.pallas import tpu as pltpu
from jax.sharding import Mesh, PartitionSpec as P

DH = 128
BLOCK = 128
GROUP = 8
CHIPS = 4
STEPS = (0, 2, 3, 1)
HALF = CHIPS * 128
MID = GROUP - 2
TOKENS = GROUP * BLOCK
COARSE = TOKENS // 2 + TOKENS // 4 + TOKENS // 8
START = {1: 0, 2: TOKENS // 2, 3: TOKENS // 2 + TOKENS // 4}
EPS = 1e-06
FLOOR = -1e30
FLOPS = 10**8
SCALE = 1.0 / math.sqrt(DH)
SHARP = SCALE * math.log2(math.e)
VMEM = pl.BlockSpec(memory_space=pltpu.VMEM)
HBM = pl.BlockSpec(memory_space=pltpu.HBM)
F32 = jnp.float32
BF16 = jnp.bfloat16


def call(kernel, outs, ins, scratch=(), flops=0, vmem=16):
    return pl.pallas_call(
        kernel,
        out_shape=[jax.ShapeDtypeStruct(*out[:2]) for out in outs],
        in_specs=[VMEM] * ins if isinstance(ins, int) else ins,
        out_specs=[out[2] if len(out) > 2 else VMEM for out in outs],
        scratch_shapes=[pltpu.VMEM(*one) if isinstance(one, tuple) else one for one in scratch],
        compiler_params=pltpu.CompilerParams(vmem_limit_bytes=vmem * 1024 * 1024),
        cost_estimate=pl.CostEstimate(flops=flops, bytes_accessed=0, transcendentals=0),
    )


def run_all(copies):
    for copy in copies:
        copy.start()
    for copy in copies:
        copy.wait()


def at_block(b):
    return pl.ds(pl.multiple_of(b * BLOCK, BLOCK), BLOCK)


def rows(b, n=1):
    return pl.ds(b * BLOCK, n * BLOCK)


def nt(a, b):
    return lax.dot_general(a, b, (((1,), (1,)), ((), ())), preferred_element_type=F32)


def nn(a, b):
    return lax.dot_general(a, b, (((1,), (0,)), ((), ())), preferred_element_type=F32)


def tn(a, b):
    return lax.dot_general(a, b, (((0,), (0,)), ((), ())), preferred_element_type=F32)


def pack_kernel(x, y, got_x, got_y, *messages):
    core, chip = lax.axis_index("c"), lax.axis_index("x")
    mine, theirs = at_block(core), at_block(1 - core)
    for step, message in zip(STEPS, messages):
        here = (chip ^ step) * DH
        cols = pl.ds(pl.multiple_of(core * HALF + here, DH), DH)
        for i, (own, got) in enumerate(((x, got_x), (y, got_y))):
            message[i, mine, :] = own[:, pl.ds(pl.multiple_of(here, DH), DH)]
            message[i, theirs, :] = got[:, cols]


def places():
    chip = lax.axis_index("x")
    return [pl.ds(pl.multiple_of((chip ^ step) * 2 * BLOCK, BLOCK), 2 * BLOCK) for step in STEPS]


def pool(x, p, f32):
    f32[...] = x[...].astype(F32)
    n = TOKENS
    for level in (1, 2, 3):
        n //= 2
        pooled = f32[pl.ds(0, n, 2), :] + f32[pl.ds(1, n, 2), :]
        p[pl.ds(START[level], n), :] = (pooled * 0.5**level).astype(BF16)
        f32[pl.ds(0, n), :] = pooled


def keys_kernel(*refs):
    parts, (k, v, kp, vp, pair, other, f32) = refs[:CHIPS], refs[CHIPS:]
    odd = lax.rem(lax.axis_index("z"), 2)
    for part, at in zip(parts, places()):
        k[at, :] = part[0]
        v[at, :] = part[1]
    pool(k, kp, f32)
    pool(v, vp, f32)
    near, far = at_block((1 - odd) * (GROUP - 1)), at_block(odd * (GROUP - 1))
    pair[0] = k[near, :]
    pair[1] = v[near, :]
    pair[2] = kp[pl.ds(START[3], BLOCK), :]
    pair[3] = vp[pl.ds(START[3], BLOCK), :]
    other[0] = k[far, :]
    other[1] = v[far, :]


def queries_kernel(*refs):
    parts, (q, d, qp, f32) = refs[:CHIPS], refs[CHIPS:]
    for part, at in zip(parts, places()):
        q[at, :] = part[0]
        d[at, :] = part[1]
    pool(q, qp, f32)


def spread(scratch, x, n, times=2):
    for j in range(times):
        scratch[pl.ds(j, n, times), :] = x
    return scratch[pl.ds(0, n * times), :]


def column(x):
    return jnp.sum(x, axis=1, keepdims=True)


def attend(items, tops, totals, sums):
    scores = []
    for queries, keys, _, _, invalid in items:
        one = nt(queries, keys)
        if invalid is not None:
            side, bad = invalid
            lane = lax.broadcasted_iota(jnp.int32, one.shape, 1) // BLOCK
            one = jnp.where((lane == side) & bad, FLOOR, one)
        scores.append(one)
    weights = []
    for one, (_, _, _, at, _) in zip(scores, items):
        top = jnp.max(one, axis=1, keepdims=True)
        tops[at, :] = jnp.broadcast_to(top, (BLOCK, DH))
        weights.append(jnp.exp2((one - top) * SHARP))
    rounded = [one.astype(BF16) for one in weights]
    for one, (_, _, values, at, _) in zip(rounded, items):
        both = nn(one, jnp.concatenate([values, jnp.ones_like(values)], axis=1))
        sums[at, :] = both[:, :DH]
        totals[at, :] = both[:, DH:]
    return rounded


def forward_inner_kernel(q, k, v, qp, kp, vp, w_mid, w_coarse, tops, totals, sums):
    inner = [
        (q[rows(b + 1), :], k[rows(b, 3), :], v[rows(b, 3), :], rows(b), None) for b in range(MID)
    ]
    for b, one in enumerate(attend(inner, tops, totals, sums)):
        w_mid[rows(b), :] = one
    coarse = [
        (qp[rows(c), :], kp[rows(c ^ 1), :], vp[rows(c ^ 1), :], rows(MID + c), None) for c in range(6)
    ]
    for c, one in enumerate(attend(coarse, tops, totals, sums)):
        w_coarse[rows(c), :] = one


def forward_edge_kernel(
    q, k, v, d, qp, pair, other, gain, tops, totals, sums,
    attn, stats, w_edge, w_top, share, share1, share2, edge_k, edge_v,
    e_tops, e_totals, e_sums, up_m, up_t, up_s,
):
    z = lax.axis_index("z")
    odd = lax.rem(z, 2) == 1
    for x, edge, i in ((k, edge_k, 0), (v, edge_v, 1)):
        edge[0, rows(0), :] = jnp.where(odd, pair[i], other[i])
        edge[0, rows(1, 2), :] = x[rows(0, 2), :]
        edge[1, rows(0, 2), :] = x[rows(GROUP - 2, 2), :]
        edge[1, rows(2), :] = jnp.where(odd, other[i], pair[i])
    last = z == lax.axis_size("z") - 1
    top3 = rows(2)
    items = [
        (q[rows(b), :], edge_k[e], edge_v[e], rows(e), invalid)
        for e, (b, invalid) in enumerate(((0, (0, z == 0)), (GROUP - 1, (2, last))))
    ]
    items.append((qp[rows(6), :], pair[2], pair[3], top3, None))
    w_edge[rows(0), :], w_edge[rows(1), :], w_top[...] = attend(items, e_tops, e_totals, e_sums)
    m, t, s = e_tops[top3, :], e_totals[top3, :] * 8.0, e_sums[top3, :] * 8.0
    n = TOKENS // 8
    for level, out in ((2, share2), (1, share1)):
        em, et, es = spread(up_m, m, n), spread(up_t, t, n), spread(up_s, s, n)
        n *= 2
        at = pl.ds(MID * BLOCK + START[level], n)
        own = tops[at, :]
        m = jnp.maximum(own, em)
        here = 2.0**level * jnp.exp2((own - m) * SHARP)
        up = jnp.exp2((em - m) * SHARP)
        t = here * totals[at, :] + up * et
        s = here * sums[at, :] + up * es
        out[0] = here
        out[1] = up
    spread(up_m, m, n), spread(up_t, t, n), spread(up_s, s, n)
    lane = lax.broadcasted_iota(jnp.int32, (BLOCK, DH), 1)
    columns = jnp.zeros((BLOCK, DH), F32)
    for b in range(GROUP):
        if b in (0, GROUP - 1):
            at, (mm, tt, ss) = rows(b // (GROUP - 1)), (e_tops, e_totals, e_sums)
        else:
            at, (mm, tt, ss) = rows(b - 1), (tops, totals, sums)
        own, em = mm[at, :], up_m[rows(b), :]
        m = jnp.maximum(own, em)
        here, up = jnp.exp2((own - m) * SHARP), jnp.exp2((em - m) * SHARP)
        inverse = 1.0 / (here * tt[at, :] + up * up_t[rows(b), :])
        here, up = here * inverse, up * inverse
        rounded = (here * ss[at, :] + up * up_s[rows(b), :]).astype(BF16)
        share[0, rows(b), :] = here
        share[1, rows(b), :] = up
        attn[rows(b), :] = rounded
        flat = rounded.astype(F32)
        scaled = d[rows(b), :].astype(F32) * gain[...]
        for i, one in enumerate((column(flat * flat), column(scaled * flat))):
            columns = jnp.where(lane == i * GROUP + b, one, columns)
    turned = columns.T[: 2 * GROUP].astype(BF16)
    stats[...] = jnp.broadcast_to(turned[None], stats.shape)


def slopes_of(items):
    pressures = [nt(grad, values) for grad, values, _, _ in items]
    slopes = []
    for pressure, (_, values, weights, offset) in zip(pressures, items):
        wide = jnp.concatenate([offset] * (values.shape[0] // BLOCK), axis=1)
        slopes.append((weights.astype(F32) * (pressure - wide)).astype(BF16))
    return slopes


def backward_edge_kernel(
    features,
    stats, d, gain, attn, share, share1, share2, q, qp, pair, edge_k, edge_v, w_edge, w_top,
    out, pair_out, other_out, g0, gc, off0, offc, sl_edge, q_edge, q_top,
    buf, buf2,
):
    odd = lax.rem(lax.axis_index("z"), 2) == 1
    sums = jnp.sum(stats[...].astype(F32), axis=0) * (1.0 / features)
    sums = sums.reshape(2, GROUP, BLOCK)
    inv_row = lax.rsqrt(sums[0] + EPS)
    drop_row = inv_row * inv_row * inv_row * sums[1]
    for b in range(GROUP):
        inv = jnp.broadcast_to(inv_row[b : b + 1], (BLOCK, DH)).T
        drop = jnp.broadcast_to(drop_row[b : b + 1], (BLOCK, DH)).T
        flat = attn[rows(b), :].astype(F32)
        out[rows(b), :] = (flat * (inv * gain[...])).astype(BF16)
        scaled = d[rows(b), :].astype(F32) * gain[...]
        grad = (inv * scaled - flat * drop).astype(BF16).astype(F32)
        dot = jnp.broadcast_to(column(grad * flat), (BLOCK, DH))
        here, up = share[0, rows(b), :], share[1, rows(b), :]
        g0[rows(b), :] = (here * grad).astype(BF16)
        off0[rows(b), :] = here * dot
        buf[rows(b), :] = up * grad
        buf2[rows(b), :] = up * dot
    n = TOKENS
    for level, sh in ((1, share1), (2, share2), (3, None)):
        n //= 2
        g = buf[pl.ds(0, n, 2), :] + buf[pl.ds(1, n, 2), :]
        o = buf2[pl.ds(0, n, 2), :] + buf2[pl.ds(1, n, 2), :]
        at = pl.ds(START[level], n)
        if sh is None:
            gc[at, :] = (g * 8.0).astype(BF16)
            offc[at, :] = o * 8.0
        else:
            here, up = sh[0], sh[1]
            gc[at, :] = (g * here).astype(BF16)
            offc[at, :] = o * here
            buf[pl.ds(0, n), :] = g * up
            buf2[pl.ds(0, n), :] = o * up
    items = [
        (g0[rows(b), :], edge_v[e], w_edge[rows(e), :], off0[rows(b), :])
        for e, b in ((0, 0), (1, GROUP - 1))
    ]
    top_grad = gc[rows(6), :]
    items.append((top_grad, pair[3], w_top[...], offc[rows(6), :]))
    slopes = slopes_of(items)
    edges = []
    for e, b in ((0, 0), (1, GROUP - 1)):
        sl_edge[rows(e), :] = slopes[e]
        q_edge[rows(e), :] = nn(slopes[e], edge_k[e]) * SCALE
        side = slice(2 * e * BLOCK, (2 * e + 1) * BLOCK)
        edges.append((
            (tn(slopes[e][:, side], q[rows(b), :]) * SCALE).astype(BF16),
            tn(w_edge[rows(e), side], items[e][0]).astype(BF16),
        ))
    q_top[...] = nn(slopes[2], pair[2]) * SCALE
    pair_out[2] = (tn(slopes[2], qp[rows(6), :]) * SCALE).astype(BF16)
    pair_out[3] = tn(w_top[...], top_grad).astype(BF16)
    for i in range(2):
        pair_out[i] = jnp.where(odd, edges[0][i], edges[1][i])
        other_out[i] = jnp.where(odd, edges[1][i], edges[0][i])


def backward_inner_kernel(
    q, k, v, qp, kp, vp, w_mid, w_coarse, w_edge, g0, gc, off0, offc, sl_edge, q_edge, q_top, out,
    pair, other, k_grad, v_grad, m0, m1, m2, m3, pair_out, other_out,
    sl_mid, sl_coarse, buf, grads, q_grad,
):
    coarse = slopes_of([
        (gc[rows(c), :], vp[rows(c ^ 1), :], w_coarse[rows(c), :], offc[rows(c), :]) for c in range(6)
    ])
    for c, slope in enumerate(coarse):
        sl_coarse[rows(c), :] = slope
        grads[rows(c), :] = nn(slope, kp[rows(c ^ 1), :]) * SCALE
    inner = slopes_of([
        (g0[rows(b + 1), :], v[rows(b, 3), :], w_mid[rows(b), :], off0[rows(b + 1), :])
        for b in range(MID)
    ])
    for b, slope in enumerate(inner):
        sl_mid[rows(b), :] = slope
    e = grads[rows(4, 2), :] * 0.25 + spread(buf, q_top[...] * 0.125, 128)
    e = grads[rows(0, 4), :] * 0.5 + spread(buf, e, 256)
    spread(buf, e, 512)
    for b in range(GROUP):
        if b in (0, GROUP - 1):
            part = q_edge[rows(b // (GROUP - 1)), :]
        else:
            part = nn(inner[b - 1], k[rows(b - 1, 3), :]) * SCALE
        q_grad[rows(b), :] = (part + buf[rows(b), :]).astype(BF16)

    pair_out[...] = pair[...]
    other_out[...] = other[...]
    for at, message in zip(places(), (m0, m1, m2, m3)):
        message[0] = out[at, :]
        message[1] = q_grad[at, :]

    def key_value(factor, edge, mid, mid_c, right, right_c, res):
        for c in range(6):
            grads[rows(c ^ 1), :] = tn(mid_c[rows(c), :], right_c[rows(c), :])
        e = grads[rows(4, 2), :] * (0.25 * factor)
        e = grads[rows(0, 4), :] * (0.5 * factor) + spread(buf, e, 256)
        spread(buf, e, 512)
        for j in range(GROUP):
            lefts, rights = [], []
            for side in range(3):
                b = j + 1 - side
                cols = pl.ds(side * BLOCK, BLOCK)
                if b in (0, GROUP - 1):
                    lefts.append(edge[rows(b // (GROUP - 1)), cols])
                elif 0 < b < GROUP - 1:
                    lefts.append(mid[rows(b - 1), cols])
                else:
                    continue
                rights.append(right[rows(b), :])
            total = tn(jnp.concatenate(lefts, axis=0), jnp.concatenate(rights, axis=0))
            res[rows(j), :] = total * factor + buf[rows(j), :]

    key_value(SCALE, sl_edge, sl_mid, sl_coarse, q, qp, k_grad)
    key_value(1.0, w_edge, w_mid, w_coarse, g0, gc, v_grad)


def collect_kernel(k_grad, v_grad, pair, other, *refs):
    messages, buf = refs[:-1], refs[-1]
    odd = lax.rem(lax.axis_index("z"), 2) == 1
    for i, x in enumerate((k_grad, v_grad)):
        spread(buf, pair[2 + i].astype(F32) * 0.125, 128, 8)
        buf[...] += x[...]
        buf[rows(0), :] += jnp.where(odd, pair[i], other[i]).astype(F32)
        buf[rows(GROUP - 1), :] += jnp.where(odd, other[i], pair[i]).astype(F32)
        for at, message in zip(places(), messages):
            message[i] = buf[at, :].astype(BF16)


def regroup_kernel(*refs):
    parts, (own, away) = refs[:CHIPS], refs[CHIPS:]
    core, chip = lax.axis_index("c"), lax.axis_index("x")
    mine, theirs = at_block(core), at_block(1 - core)
    for step, part in zip(STEPS, parts):
        cols = pl.ds(pl.multiple_of((chip ^ step) * DH, DH), DH)
        for i in range(2):
            own[i, :, cols] = part[i, mine, :]
            away[i, :, cols] = part[i, theirs, :]


def finish_kernel(own, got, *refs):
    results, sem = refs[:-1], refs[-1]
    core = lax.axis_index("c")
    copies = []
    for i, x in enumerate(results):
        for j, (half, source) in enumerate(((1 - core, got), (core, own))):
            cols = pl.ds(pl.multiple_of(half * HALF, HALF), HALF)
            copies.append(pltpu.make_async_copy(source.at[i], x.at[:, cols], sem.at[j, i]))
    run_all(copies)


def swap_pair(x):
    return lax.ppermute(x, "z", [(i, i ^ 1) for i in range(lax.axis_size("z"))])


def swap_other(x):
    up = [(i, i + 1) for i in range(1, lax.axis_size("z") - 1, 2)]
    return lax.ppermute(x, "z", up + [(target, source) for source, target in up])


def swap_core(x):
    return lax.ppermute(x, "c", [(0, 1), (1, 0)])


def swap_chips(messages):
    return [messages[0]] + [
        lax.ppermute(message, "x", [(i, i ^ step) for i in range(CHIPS)])
        for step, message in zip(STEPS[1:], messages[1:])
    ]


def exchange(x, axes):
    return lax.all_to_all(x, axes, 0, 0, tiled=True)


def local(query, keys, values, gain, out_grad):
    token = ((BLOCK, query.shape[1]), BF16, HBM)
    part = ((2, 2 * BLOCK, DH), BF16)
    half = ((2, BLOCK, HALF), BF16)
    partners = GROUP * lax.axis_size("head")
    message = ((4, BLOCK, DH), BF16)
    edge = ((2, BLOCK, DH), BF16)
    whole = ((TOKENS, DH), BF16)
    whole_f = ((TOKENS, DH), F32)
    coarse = ((COARSE, DH), BF16)
    coarse_f = ((COARSE, DH), F32)
    one_f = ((BLOCK, DH), F32)
    two_f = ((2 * BLOCK, DH), F32)
    w_mids = ((MID * BLOCK, 3 * BLOCK), BF16)
    w_coarses = ((6 * BLOCK, BLOCK), BF16)
    w_edges = ((2 * BLOCK, 3 * BLOCK), BF16)
    w_tops = ((BLOCK, BLOCK), BF16)
    inner_f = (((MID + 6) * BLOCK, DH), F32)
    edge_sets = ((2, 3 * BLOCK, DH), BF16)
    shares = [((2, TOKENS >> level, DH), F32) for level in range(3)]
    features = query.shape[1] * lax.axis_size("head")

    head = lax.axis_index("c") * CHIPS + lax.axis_index("x")
    my_gain = lax.dynamic_slice_in_dim(gain, head * DH, DH).reshape(1, DH)

    def send(x, y):
        gots = [swap_core(one) for one in (x, y)]
        own = [lax.dynamic_slice_in_dim(one, lax.axis_index("c") * HALF, HALF, 1) for one in (x, y)]
        return swap_chips(call(pack_kernel, [part] * CHIPS, 4)(*own, *gots))

    got_keys = send(keys, values)
    got_queries = send(query, out_grad)
    k, v, kp, vp, pair, other = call(
        keys_kernel, [whole] * 2 + [coarse] * 2 + [message, edge], CHIPS, [whole_f]
    )(*got_keys)
    pair, other = swap_pair(pair), swap_other(other)
    q, d, qp = call(queries_kernel, [whole] * 2 + [coarse], CHIPS, [whole_f])(*got_queries)
    w_mid, w_coarse, *inner = call(
        forward_inner_kernel, [w_mids, w_coarses] + [inner_f] * 3, 6, flops=FLOPS
    )(q, k, v, qp, kp, vp)
    attn, stats, w_edge, w_top, share, share1, share2, edge_k, edge_v = call(
        forward_edge_kernel,
        [whole, ((partners, 2 * GROUP, DH), BF16), w_edges, w_tops] + shares + [edge_sets] * 2,
        11,
        [((3 * BLOCK, DH), F32)] * 3 + [whole_f] * 3,
    )(q, k, v, d, qp, pair, other, my_gain, *inner)
    stats = exchange(stats, ("x", "c", "head"))

    def backward_edge(*refs):
        backward_edge_kernel(features, *refs)

    out, pair_back, other_back, g0, gc, off0, offc, sl_edge, q_edge, q_top = call(
        backward_edge,
        [whole, message, edge, whole, coarse, whole_f, coarse_f, w_edges, two_f, one_f],
        14,
        [whole_f] * 2,
    )(stats, d, my_gain, attn, share, share1, share2, q, qp, pair, edge_k, edge_v, w_edge, w_top)
    k_grad, v_grad, *messages, pair_back, other_back = call(
        backward_inner_kernel,
        [whole_f, whole_f] + [part] * CHIPS + [message, edge],
        19,
        [w_mids, w_coarses, whole_f, coarse_f, whole],
        flops=2 * FLOPS,
    )(q, k, v, qp, kp, vp, w_mid, w_coarse, w_edge, g0, gc, off0, offc, sl_edge, q_edge, q_top, out,
      pair_back, other_back)
    pair_back, other_back = swap_pair(pair_back), swap_other(other_back)

    def deliver(messages):
        own, away = call(regroup_kernel, [half] * 2, CHIPS)(*swap_chips(messages))
        finish = call(finish_kernel, [token] * 2, 2, [pltpu.SemaphoreType.DMA((2, 2))])
        return finish(own, swap_core(away))

    out, q_grad = deliver(messages)
    messages = call(collect_kernel, [part] * CHIPS, 4, [whole_f])(k_grad, v_grad, pair_back, other_back)
    return (out, q_grad, *deliver(messages))


def solution(mesh):
    chips = (CHIPS, 2)
    axes = ("z", "x", "c", "head")
    heads = mesh.shape["head"]
    fine = Mesh(mesh.devices.reshape((mesh.shape["seq"] // GROUP, *chips, heads)), axes)
    spec = P(("z", "x", "c"), "head")
    in_specs = (spec, spec, spec, P("head"), spec)
    return jax.shard_map(
        local, mesh=fine, in_specs=in_specs, out_specs=(spec,) * 4, check_vma=False
    )
```
